256 devices in a mesh: side: 2 (over core), seq: 16 (over x, y), tensor: 8 (over z).
Axes of the slice: x: 4, y: 4, z: 8, core: 2. Of those that a mesh axis runs over, the one named last changes fastest.
Arguments:
- x_rows: bfloat16 [512, 8192], P(('side', 'seq')), may hold values from -40 to 40
- attn_gain: bfloat16 [8192], replicated, may hold values from 0.25 to 1.75
- final_gain: bfloat16 [8192], replicated, may hold values from 0.25 to 1.75
- w_query: bfloat16 [8192, 8192], P(('side', 'seq'), 'tensor'), may hold values from -0.0625 to 0.0625
- w_kv: bfloat16 [8192, 2, 1024], P(('side', 'seq'), None, 'tensor'), may hold values from -0.15625 to 0.15625
- w_out: bfloat16 [8192, 8192], P('tensor', ('side', 'seq')), may hold values from -0.0625 to 0.0625
- kv_cache: bfloat16 [2, 4, 32768, 1024], P(None, None, ('side', 'seq'), 'tensor'), may hold values from -1500 to 1500
- w_vocab: bfloat16 [8192, 152064], P(None, ('side', 'seq', 'tensor')), may hold values from -16 to 16
- token_ids: int32 [512], replicated, may hold values from 0 to 152063
- cache_len: int32 [4], replicated, may hold values from 8192 to 32768, as said below
- row_traj: int32 [512], replicated, may hold values from 0 to 3, as said below
Outputs:
- attended: bfloat16 [512, 8192], P('tensor', ('side', 'seq'))
- logprob: float32 [512], replicated
The draws below stay inside these ranges and needn't reach their ends.
Inputs may be any that keep to these rules, and one draw needn't show every extreme that they name: `row_traj`: each of the 4 trajectories owns exactly 128 rows. `cache_len`: at least one trajectory's cache is full.
All inputs are finite; a program needn't handle non-finite values.
Results may differ from the reference program's by a relative error of at most 0.02.
Values may be sent and summed in bfloat16 or wider, within the bound.
A program may use at most 192 MiB of HBM per device.

```python
import math
import jax
import jax.numpy as jnp
import numpy as np
from jax import lax

D = 8192
H = 64
KVH = 8
HD = 128
VOCAB = 152064
TRAJ = 4
STEPS = 128
CACHE_DEV = 1024
ROWS = 512
CACHE = 32768


def draw_x_rows(key, part):
    key = jax.random.fold_in(key, 1)
    first_key, second_key, third_key = jax.random.split(key, 3)
    base = jax.random.normal(first_key, (ROWS, D), jnp.float32)
    row_scale = jnp.exp(jax.random.uniform(second_key, (ROWS, 1), jnp.float32, 0.0, math.log(10.0))) * 0.3
    col_scale = jnp.exp(jax.random.uniform(third_key, (1, D), jnp.float32, 0.0, math.log(10.0))) * 0.3
    return jnp.clip(base * row_scale * col_scale, -40.0, 40.0).astype(jnp.bfloat16)


def draw_kv_cache(key, part):
    key = jax.random.fold_in(key, 2)
    first_key = jax.random.fold_in(key, 0)
    shape = (2, TRAJ, CACHE, KVH * HD)
    values = jnp.clip(jax.random.normal(first_key, shape, jnp.float32) * 2.5, -15.0, 15.0)
    return values.astype(jnp.bfloat16)


def draw_w_vocab(key, part):
    key = jax.random.fold_in(key, 3)
    first_key, second_key = jax.random.split(key, 2)
    base = jax.random.normal(first_key, (D, VOCAB), jnp.float32)
    col_scale = jnp.exp(jax.random.uniform(second_key, (1, VOCAB), jnp.float32, 0.0, math.log(10.0)))
    values = base * col_scale * (1.2 / math.sqrt(D))
    return jnp.clip(values, -16.0, 16.0).astype(jnp.bfloat16)


def draw_cache_len(key, part):
    key = jax.random.fold_in(key, 4)
    first_key, second_key = jax.random.split(key)
    lengths = jax.random.randint(first_key, (TRAJ,), CACHE // 4, CACHE + 1)
    full_one = jax.random.randint(second_key, (), 0, TRAJ)
    return jnp.where(jnp.arange(TRAJ) == full_one, CACHE, lengths).astype(jnp.int32)


def draw_row_traj(key, part):
    key = jax.random.fold_in(key, 5)
    owners = jnp.arange(TRAJ * STEPS, dtype=jnp.int32) // STEPS
    return jax.random.permutation(key, owners).astype(jnp.int32)


def plant(array, own_key, least, top_value):
    dims = array.shape
    spot = [jax.random.randint(jax.random.fold_in(own_key, axis), (), 0, dims[axis]) for axis in range(len(dims))]
    array = array.at[tuple(spot)].set(least)
    longest = dims.index(max(dims))
    spot[longest] = (spot[longest] + 1) % dims[longest]
    return array.at[tuple(spot)].set(top_value)


def shard_levels(rng, shape, cuts, low, high):
    def one(axis_at, shards_of):
        steps = jax.random.uniform(jax.random.fold_in(jax.random.fold_in(rng, 6), axis_at), (shards_of,), jnp.float32, low / len(cuts), high / len(cuts))
        return jnp.repeat(jnp.exp(steps), shape[axis_at] // shards_of).reshape((-1,) + (1,) * (len(shape) - axis_at - 1))

    gain = one(*cuts[0])
    for cut in cuts[1:]:
        gain = gain * one(*cut)
    return gain


def wide_ids(stream_key, extent, amount, lean):
    weights = [min(1 << octave, amount + 1 - (1 << octave)) * (1 << 20) // math.isqrt((1 << octave) ** lean) + 1 for octave in range((amount + 1).bit_length()) if 1 << octave <= amount]
    scale = 1 + sum(weights) // (1 << 30)
    listing = np.cumsum(np.array([max(1, weight // scale) for weight in weights]))
    pick = jax.random.randint(jax.random.fold_in(stream_key, 1), extent, 0, int(listing[len(weights) - 1]))
    start = jnp.left_shift(1, jnp.searchsorted(jnp.asarray(listing, jnp.int32), pick, side="right").astype(jnp.int32))
    grade = start - 1 + jax.random.randint(jax.random.fold_in(stream_key, 4), extent, 0, 1 << 30) % jnp.minimum(start, amount + 1 - start)
    return jax.random.permutation(jax.random.fold_in(stream_key, 2), amount)[grade].astype(jnp.int32)


def normal_values(rng, dims, scale, limit, shards=(), kind=jnp.bfloat16):
    entries = jax.random.normal(rng, dims, jnp.float32) * scale
    if len(shards) > 0:
        entries = shard_levels(rng, dims, shards, -0.22, 0.18) * entries
    return jnp.clip(entries, min=-limit, max=limit).astype(kind)


def setup_inputs(seed: int = 0) -> dict:
    key_of = jax.random.split(jax.random.key(seed), 12)
    x_rows = draw_x_rows(jax.random.fold_in(key_of[11], 71), 0)
    attn_gain = jnp.clip(1.0 + 0.15 * jax.random.normal(key_of[1], (D,), jnp.float32), 0.25, 1.75).astype(jnp.bfloat16)
    final_gain = jnp.clip(1.0 + 0.15 * jax.random.normal(key_of[2], (D,), jnp.float32), 0.25, 1.75).astype(jnp.bfloat16)
    w_query = normal_values(key_of[3], (D, H * HD), D ** -0.5, 0.0625, ((0, 32), (1, 8)))
    w_kv = normal_values(key_of[4], (D, 2, KVH * HD), (D * 4 // 25) ** -0.5, 0.15625, ((0, 32), (2, 8)))
    w_out = normal_values(key_of[5], (H * HD, D), (H * HD) ** -0.5, 0.0625, ((0, 8), (1, 32)))
    kv_cache = draw_kv_cache(jax.random.fold_in(key_of[11], 71), 0)
    w_vocab = draw_w_vocab(jax.random.fold_in(key_of[11], 71), 0)
    token_ids = plant(wide_ids(key_of[8], (ROWS,), VOCAB, 2), jax.random.fold_in(key_of[8], 3), 0, VOCAB - 1).astype(jnp.int32)
    cache_len = draw_cache_len(jax.random.fold_in(key_of[11], 71), 0)
    row_traj = draw_row_traj(jax.random.fold_in(key_of[11], 71), 0)
    return {"x_rows": x_rows, "attn_gain": attn_gain, "final_gain": final_gain, "w_query": w_query, "w_kv": w_kv, "w_out": w_out, "kv_cache": kv_cache, "w_vocab": w_vocab, "token_ids": token_ids, "cache_len": cache_len, "row_traj": row_traj}


epsilon = 1e-06
rope_base = 1000000.0
masked_low = -1e+30

def rms_scale(rows_in, gain_vec):
    values = rows_in.astype(jnp.float32)
    mean_sq = lax.optimization_barrier(jnp.mean(values * values, axis=-1, keepdims=True))
    return (values * lax.rsqrt(mean_sq + epsilon) * gain_vec.astype(jnp.float32)).astype(jnp.bfloat16)

def row_places(row_traj, cache_len, traj_count):
    member = (row_traj[:, None] == jnp.arange(traj_count, dtype=jnp.int32)[None, :]).astype(jnp.int32)
    running = jnp.cumsum(member, axis=0)
    step_index = lax.optimization_barrier(jnp.sum(running * member, axis=1)) - 1
    places = lax.optimization_barrier(jnp.sum(member * cache_len[None, :], axis=1)) + step_index
    return (step_index, places)

def rope_angles(places, head_dim):
    half_dim = head_dim // 2
    spread = jnp.exp(jnp.arange(half_dim).astype(jnp.float32) * (-2.0 * math.log(rope_base) / head_dim))
    return places.astype(jnp.float32)[:, None, None] * spread[None, None, :]

def rotate_half(values, angles):
    half_dim = values.shape[-1] // 2
    cosine = jnp.cos(angles)
    sine_part = jnp.sin(angles)
    leading = values[..., :half_dim]
    trailing = values[..., half_dim:]
    return jnp.concatenate([leading * cosine - trailing * sine_part, trailing * cosine + leading * sine_part], axis=-1)

def block_terms(queries, keys_block, values_block, allowed, scale):
    scores = jnp.einsum('bskgd,bpkd->bskgp', queries.astype(jnp.float32), keys_block.astype(jnp.float32)) * scale
    peak_score = lax.optimization_barrier(jnp.max(jnp.where(allowed, scores, masked_low), axis=-1))
    weights = jnp.where(allowed, jnp.exp(scores - peak_score[..., None]), 0.0)
    weight_sum = lax.optimization_barrier(jnp.sum(weights, axis=-1))
    rounded = lax.optimization_barrier(weights.astype(jnp.bfloat16))
    block_out = jnp.einsum('bskgp,bpkd->bskgd', rounded.astype(jnp.float32), values_block.astype(jnp.float32))
    return (peak_score, weight_sum, block_out)

def combine(earlier, later):
    joined = jnp.maximum(earlier[0], later[0])
    first_scale = jnp.exp(earlier[0] - joined)
    second_scale = jnp.exp(later[0] - joined)
    return (joined, earlier[1] * first_scale + later[1] * second_scale, earlier[2] * first_scale[..., None] + later[2] * second_scale[..., None])

def reference(x_rows, attn_gain, final_gain, w_query, w_kv, w_out, kv_cache, w_vocab, token_ids, cache_len, row_traj):
    row_count = x_rows.shape[0]
    group_size = H // KVH
    normed = rms_scale(x_rows, attn_gain)
    query_sum = jnp.dot(normed, w_query, preferred_element_type=jnp.float32)
    pair_sum = jnp.dot(normed, w_kv.reshape(D, 2 * KVH * HD), preferred_element_type=jnp.float32)
    step_index, places = row_places(row_traj, cache_len, TRAJ)
    angles = rope_angles(places, HD)
    queries = rotate_half(query_sum.reshape(row_count, H, HD), angles).astype(jnp.bfloat16)
    pair_rows = pair_sum.reshape(row_count, 2, KVH, HD)
    new_keys = rotate_half(pair_rows[:, 0], angles).astype(jnp.bfloat16)
    new_values = pair_rows[:, 1].astype(jnp.bfloat16)
    order = jnp.argsort(row_traj, stable=True).astype(jnp.int32)
    sorted_q = queries[order].reshape(TRAJ, STEPS, KVH, group_size, HD)
    sorted_keys = new_keys[order].reshape(TRAJ, STEPS, KVH, HD)
    sorted_values = new_values[order].reshape(TRAJ, STEPS, KVH, HD)
    scale = float(HD) ** (-0.5)
    cache_keys = kv_cache[0].reshape(TRAJ, CACHE, KVH, HD)
    cache_values = kv_cache[1].reshape(TRAJ, CACHE, KVH, HD)

    def visit(state, block):
        start = block * CACHE_DEV
        keys_block = lax.dynamic_slice_in_dim(cache_keys, start, CACHE_DEV, 1)
        values_block = lax.dynamic_slice_in_dim(cache_values, start, CACHE_DEV, 1)
        positions = start + jnp.arange(CACHE_DEV, dtype=jnp.int32)
        allowed = (positions[None, :] < cache_len[:, None])[:, None, None, None, :]
        return (combine(state, block_terms(sorted_q, keys_block, values_block, allowed, scale)), None)
    initial = (jnp.full((TRAJ, STEPS, KVH, group_size), masked_low, jnp.float32), jnp.zeros((TRAJ, STEPS, KVH, group_size), jnp.float32), jnp.zeros((TRAJ, STEPS, KVH, group_size, HD), jnp.float32))
    state, unused = lax.scan(visit, initial, jnp.arange(CACHE // CACHE_DEV, dtype=jnp.int32))
    causal = (jnp.arange(STEPS)[None, :] <= jnp.arange(STEPS)[:, None])[None, :, None, None, :]
    state = combine(state, block_terms(sorted_q, sorted_keys, sorted_values, causal, scale))
    attended_sorted = (state[2] / state[1][..., None]).astype(jnp.bfloat16).reshape(row_count, H * HD)
    attn_rows = jnp.zeros((row_count, H * HD), jnp.bfloat16).at[order].set(attended_sorted)
    attended = (x_rows.astype(jnp.float32) + jnp.dot(attn_rows, w_out, preferred_element_type=jnp.float32)).astype(jnp.bfloat16)
    final_rows = rms_scale(attended, final_gain)
    logits = jnp.dot(final_rows, w_vocab, preferred_element_type=jnp.float32)
    row_peak = lax.optimization_barrier(jnp.max(logits, axis=1))
    exp_total = lax.optimization_barrier(jnp.sum(jnp.exp(logits - row_peak[:, None]), axis=1))
    picked = jnp.take_along_axis(logits, token_ids[:, None], axis=1)[:, 0]
    return (attended, picked - row_peak - jnp.log(exp_total))
```

```python
import functools
import math

import jax
import jax.numpy as jnp
from jax import lax
from jax.experimental import pallas as pl
from jax.experimental.pallas import tpu as pltpu
from jax.sharding import PartitionSpec as P

HD = 128
TRAJ = 4
MESH = pl.DeviceIdType.MESH

epsilon = 1e-06
rope_base = 1000000.0
masked_low = -1e30
SCALE2 = float(HD) ** (-0.5) * math.log2(math.e)

F32 = jnp.float32
BF16 = jnp.bfloat16


def dot(a, b):
    return jnp.dot(a, b, preferred_element_type=F32)


def dot_nt(a, b):
    return lax.dot_general(a, b, (((1,), (1,)), ((), ())), preferred_element_type=F32)


def rows(start, size):
    return pl.ds(pl.multiple_of(start, size), size)


def column(row):
    return jnp.broadcast_to(row, (128, 128)).T


def merge(parts):
    top = functools.reduce(jnp.maximum, [p[1] for p in parts])
    factors = [jnp.exp2((p[1] - top) * SCALE2) for p in parts]
    mass = sum(p[2] * f for p, f in zip(parts, factors))
    outs = [
        sum(p[0](h) * f[:, h : h + 1] for p, f in zip(parts, factors)) for h in range(8)
    ]
    return outs, top, mass


def kernel(
    x_ref,
    ag_ref,
    fg_ref,
    wq_ref,
    wkv_ref,
    wo_hbm,
    kv_hbm,
    wv_hbm,
    tok_ref,
    clen_ref,
    traj_ref,
    cos_ref,
    sin_ref,
    att_ref,
    lp_ref,
    wo,
    kv,
    wv,
    nx,
    xn,
    raw,
    place,
    place_t,
    xs,
    part,
    r1,
    s2,
    r2,
    sum2,
    r3,
    qkv,
    o_all,
    ml_all,
    rc1,
    rm1,
    sc2,
    sm2,
    rc2,
    rm2,
    oc2,
    mc2,
    rc3,
    rm3,
    ho,
    hpb,
    zs,
    zr,
    feat,
    acc,
    st,
    zt,
    fs,
    fz,
    lsem,
    bsem,
    asem,
    rawr,
    p1r,
    p2r,
    p3r,
    g1r,
    g2r,
    g3r,
    c1r,
    c2r,
    c3r,
    h1r,
    h2r,
    h3r,
    zrr,
    zgr,
    ftr,
    fbr,
    ztr,
    fzr,
):
    c = lax.axis_index("side")
    s = lax.axis_index("seq")
    z = lax.axis_index("tensor")
    j = c * 16 + s
    along = lax.div(s, 4)
    across = lax.rem(s, 4)
    a = along + c * (across - along)
    b = across + c * (along - across)
    row0 = c * 256 + a * 64 + b * 16

    def seq_of(side, a_, b_):
        straight = a_ * 4 + b_
        return straight + side * (b_ * 4 + a_ - straight)

    def blk(a_, b_):
        return c * 16 + seq_of(c, a_, b_)

    def peer(a_, b_):
        return (c, seq_of(c, a_, b_), z)

    def turn(v, k):
        return lax.rem(v + k, 4)

    sib = (1 - c, s, z)

    def send(src, dst, ssem, rsem, dev):
        pltpu.make_async_remote_copy(
            src_ref=src, dst_ref=dst, send_sem=ssem, recv_sem=rsem, device_id=dev, device_id_type=MESH
        ).start()

    def wait(ref, sem):
        pltpu.make_async_copy(ref, ref, sem).wait()

    def local(src, dst, n):
        return pltpu.make_async_copy(src, dst, lsem.at[n])

    local(kv_hbm, kv, 0).start()
    local(wo_hbm, wo, 1).start()
    local(wv_hbm, wv, 2).start()

    barrier = pltpu.get_barrier_semaphore()

    def greet(k, carry):
        i = lax.rem(j + k, 32)
        pl.semaphore_signal(barrier, inc=1, device_id=(lax.div(i, 16), lax.rem(i, 16), z), device_id_type=MESH)
        return carry

    lax.fori_loop(1, 32, greet, 0)

    def greet_z(k, carry):
        pl.semaphore_signal(barrier, inc=1, device_id=(c, s, lax.rem(z + k, 8)), device_id_type=MESH)
        return carry

    lax.fori_loop(1, 8, greet_z, 0)

    total = jnp.zeros((16, 1), F32)
    for n in range(8):
        v = x_ref[:, n * 1024 : (n + 1) * 1024].astype(F32)
        total = total + jnp.sum(v * v, axis=1, keepdims=True)
    unit = lax.rsqrt(total * (1.0 / 8192.0) + epsilon)
    for n in range(8):
        cols = slice(n * 1024, (n + 1) * 1024)
        v = x_ref[:, cols].astype(F32)
        nx[:, cols] = (v * unit * ag_ref[:, cols].astype(F32)).astype(BF16)

    pl.semaphore_wait(barrier, 38)

    def send_rows(k, carry):
        i = lax.rem(j + k, 32)
        send(
            nx.at[:, rows(i * 256, 256)],
            xn.at[rows(j * 16, 16), :],
            bsem.at[0],
            asem.at[0],
            (lax.div(i, 16), lax.rem(i, 16), z),
        )
        return carry

    lax.fori_loop(1, 32, send_rows, 0)
    xn[rows(j * 16, 16), :] = nx[:, rows(j * 256, 256)]

    quarter = lax.rem(j, 4)
    holds_raw = lax.div(j, 4) == z

    @pl.when(holds_raw)
    def _():
        def send_raw(k, carry):
            i = lax.rem(j + k, 32)
            send(
                x_ref.at[:, rows(i * 256, 256)],
                raw.at[rows(quarter * 16, 16), :],
                bsem.at[1],
                rawr.at[quarter],
                (lax.div(i, 16), lax.rem(i, 16), z),
            )
            return carry

        lax.fori_loop(1, 32, send_raw, 0)
        raw[rows(quarter * 16, 16), :] = x_ref[:, rows(j * 256, 256)]

    traj = traj_ref[...].astype(F32)
    traj_cols = [column(traj[g : g + 1, :]) for g in range(4)]
    sub = lax.broadcasted_iota(jnp.int32, (128, 128), 0)
    lane = lax.broadcasted_iota(jnp.int32, (128, 128), 1)
    for g in range(4):
        step_col = jnp.zeros((128, 1), F32)
        step_row = jnp.zeros((1, 128), F32)
        for e in range(g + 1):
            same = jnp.where(traj_cols[g] == traj[e : e + 1, :], 1.0, 0.0)
            if e == g:
                same = jnp.where(lane < sub, same, 0.0)
            step_col = step_col + jnp.sum(same, axis=1, keepdims=True)
            same = jnp.where(traj_cols[e] == traj[g : g + 1, :], 1.0, 0.0)
            if e == g:
                same = jnp.where(sub < lane, same, 0.0)
            step_row = step_row + jnp.sum(same, axis=0, keepdims=True)
        slot_col = traj_cols[g] * 128.0 + step_col
        slot_row = traj[g : g + 1, :] * 128.0 + step_row
        for e in range(4):
            place_t[g * 128 : (g + 1) * 128, e * 128 : (e + 1) * 128] = jnp.where(
                (lane + e * 128).astype(F32) == slot_col, 1.0, 0.0
            ).astype(BF16)
            place[e * 128 : (e + 1) * 128, g * 128 : (g + 1) * 128] = jnp.where(
                (sub + e * 128).astype(F32) == slot_row, 1.0, 0.0
            ).astype(BF16)

    wait(xn.at[0:496], asem.at[0])

    def project(half):
        at = rows(half * 256, 256)
        xs[at, :] = dot(place[at, :], xn[...]).astype(BF16)
        part[at, 0:1024] = dot(xs[at, :], wq_ref[...])
        part[at, 1024:1280] = dot(xs[at, :], wkv_ref[...])

    project(1 - c)
    for k in (1, 2, 3, 0):
        q = turn(b, k)
        send(part.at[rows((1 - c) * 256 + q * 64, 64), :], r1.at[rows(q * 64, 64), :], bsem.at[2], p1r.at[q], sib)
    project(c)

    def pair_sum(q):
        wait(r1.at[rows(q * 64, 64), :], p1r.at[q])
        return part[rows(c * 256 + q * 64, 64), :] + r1[rows(q * 64, 64), :]

    for k in (1, 2, 3):
        q = turn(a, k)
        s2[q] = pair_sum(q).astype(BF16)
        send(s2.at[q], r2.at[a], bsem.at[3], p2r.at[a], peer(q, b))
    sum2[...] = pair_sum(a)
    for k in (3, 2, 1):
        q = turn(a, k)
        wait(r2.at[q], p2r.at[q])
        sum2[...] += r2[q].astype(F32)
    for k in (1, 2, 3):
        q = turn(b, k)
        send(sum2.at[rows(q * 16, 16), :], r3.at[b], bsem.at[4], p3r.at[b], peer(a, q))
    r3[b] = sum2[rows(b * 16, 16), :]
    for k in (3, 2, 1):
        q = turn(b, k)
        wait(r3.at[q], p3r.at[q])
    sums = (r3[0] + r3[1]) + (r3[2] + r3[3])
    cosine = cos_ref[...]
    sine = sin_ref[...]
    mine = rows(row0, 16)
    for h in range(9):
        v = sums[:, h * 128 : (h + 1) * 128]
        qkv[mine, h * 128 : (h + 1) * 128] = (v * cosine + pltpu.roll(v, 64, 1) * sine).astype(BF16)
    qkv[mine, 1152:1280] = sums[:, 1152:1280].astype(BF16)

    def spread(ref, n, r_b, r_a, r_s):
        for k in (1, 2, 3):
            send(ref.at[mine, :], ref.at[mine, :], bsem.at[n], r_b.at[b], peer(a, turn(b, k)))
        for k in (3, 2, 1):
            q = turn(b, k)
            wait(ref.at[rows(c * 256 + a * 64 + q * 16, 16), :], r_b.at[q])
        span = rows(c * 256 + a * 64, 64)
        for k in (1, 2, 3):
            send(ref.at[span, :], ref.at[span, :], bsem.at[n + 1], r_a.at[a], peer(turn(a, k), b))
        for k in (3, 2, 1):
            q = turn(a, k)
            wait(ref.at[rows(c * 256 + q * 64, 64), :], r_a.at[q])
        for n_half in (0, 1):
            span = rows(c * 256 + n_half * 128, 128)
            send(ref.at[span, :], ref.at[span, :], bsem.at[n + 2], r_s.at[n_half], sib)

    spread(qkv, 5, g1r, g2r, g3r)

    local(kv_hbm, kv, 0).wait()
    positions = j * 1024 + lax.broadcasted_iota(jnp.int32, (1, 1024), 1)

    def attend(t):
        at = rows(t * 128, 128)
        allowed = positions < clen_ref[t]
        keys = kv[0, t]
        values = kv[1, t]
        peaks = jnp.zeros((128, 128), F32)
        masses = jnp.zeros((128, 128), F32)
        for h in range(0, 8, 2):
            pair = jnp.concatenate(
                [qkv[at, h * 128 : (h + 1) * 128], qkv[at, (h + 1) * 128 : (h + 2) * 128]], axis=0
            )
            scores = jnp.where(allowed, dot_nt(pair, keys), masked_low)
            peak = jnp.max(scores, axis=1, keepdims=True)
            weights = jnp.exp2((scores - peak) * SCALE2)
            mass = jnp.sum(weights, axis=1, keepdims=True)
            out = dot(weights.astype(BF16), values)
            for e in (0, 1):
                o_all[at, (h + e) * 128 : (h + e + 1) * 128] = out[e * 128 : (e + 1) * 128]
                peaks = jnp.where(lane == h + e, peak[e * 128 : (e + 1) * 128], peaks)
                masses = jnp.where(lane == h + e, mass[e * 128 : (e + 1) * 128], masses)
        ml_all[0, at, :] = peaks
        ml_all[1, at, :] = masses

    def attend_own(n, carry):
        attend(c * 2 + n)
        return carry

    lax.fori_loop(0, 2, attend_own, 0)

    def attend_other(n, carry):
        t = (1 - c) * 2 + n
        wait(qkv.at[rows(t * 128, 128), :], g3r.at[n])
        attend(t)
        at = rows(t * 128, 128)
        to = rows(n * 128, 128)
        send(o_all.at[at, :], rc1.at[to, :], bsem.at[8], c1r.at[n], sib)
        send(ml_all.at[:, at, :], rm1.at[:, to, :], bsem.at[9], c1r.at[n + 2], sib)
        return carry

    lax.fori_loop(0, 2, attend_other, 0)

    def join_pair(q):
        at = rows(c * 256 + q * 64, 64)
        to = rows(q * 64, 64)
        return merge(
            [
                (lambda h: o_all[at, h * 128 : (h + 1) * 128], ml_all[0, at, :], ml_all[1, at, :]),
                (lambda h: rc1[to, h * 128 : (h + 1) * 128], rm1[0, to, :], rm1[1, to, :]),
            ]
        )

    for n in (0, 1):
        wait(rc1.at[rows(n * 128, 128), :], c1r.at[n])
        wait(rm1.at[:, rows(n * 128, 128), :], c1r.at[n + 2])
    for k in (1, 2, 3):
        q = turn(a, k)
        outs, top, mass = join_pair(q)
        for h in range(8):
            sc2[q, :, h * 128 : (h + 1) * 128] = outs[h].astype(BF16)
        sm2[q, 0] = top
        sm2[q, 1] = mass
        send(sc2.at[q], rc2.at[a], bsem.at[10], c2r.at[a], peer(q, b))
        send(sm2.at[q], rm2.at[a], bsem.at[11], c2r.at[a + 4], peer(q, b))
    outs, top, mass = join_pair(a)
    for h in range(8):
        oc2[:, h * 128 : (h + 1) * 128] = outs[h]
    mc2[0] = top
    mc2[1] = mass

    own_traj = lax.div(row0, 128)
    own_step = lax.rem(row0, 128)
    own_rows = rows(own_traj * 128, 128)
    own_q = jnp.concatenate([qkv[mine, h * 128 : (h + 1) * 128] for h in range(8)], axis=0)
    own_scores = dot_nt(own_q, qkv[own_rows, 1024:1152])
    own_scores = jnp.where(lane <= own_step + (sub & 15), own_scores, masked_low)
    own_peak = jnp.max(own_scores, axis=1, keepdims=True)
    own_weights = jnp.exp2((own_scores - own_peak) * SCALE2)
    own_mass = jnp.sum(own_weights, axis=1, keepdims=True)
    own_out = dot(own_weights.astype(BF16), qkv[own_rows, 1152:1280])
    own_peaks = jnp.zeros((16, 128), F32)
    own_masses = jnp.zeros((16, 128), F32)
    lane16 = lane[0:16]
    for h in range(8):
        own_peaks = jnp.where(lane16 == h, own_peak[h * 16 : (h + 1) * 16], own_peaks)
        own_masses = jnp.where(lane16 == h, own_mass[h * 16 : (h + 1) * 16], own_masses)

    def arrived(k):
        q = turn(a, k)
        wait(rc2.at[q], c2r.at[q])
        wait(rm2.at[q], c2r.at[q + 4])
        return (lambda h: rc2[q, :, h * 128 : (h + 1) * 128].astype(F32), rm2[q, 0], rm2[q, 1])

    parts = [(lambda h: oc2[:, h * 128 : (h + 1) * 128], mc2[0], mc2[1])]
    parts += [arrived(k) for k in (3, 2, 1)]
    outs, top, mass = merge(parts)
    for h in range(8):
        oc2[:, h * 128 : (h + 1) * 128] = outs[h]
    mc2[0] = top
    mc2[1] = mass
    for k in (1, 2, 3):
        q = turn(b, k)
        send(oc2.at[rows(q * 16, 16), :], rc3.at[b], bsem.at[12], c3r.at[b], peer(a, q))
        send(mc2.at[:, rows(q * 16, 16), :], rm3.at[b], bsem.at[13], c3r.at[b + 4], peer(a, q))
    rc3[b] = oc2[rows(b * 16, 16), :]
    rm3[b] = mc2[:, rows(b * 16, 16), :]
    for k in (3, 2, 1):
        q = turn(b, k)
        wait(rc3.at[q], c3r.at[q])
        wait(rm3.at[q], c3r.at[q + 4])
    parts = [(lambda h, q=q: rc3[q, :, h * 128 : (h + 1) * 128], rm3[q, 0], rm3[q, 1]) for q in range(4)]
    parts.append((lambda h: own_out[h * 16 : (h + 1) * 16], own_peaks, own_masses))
    outs, top, mass = merge(parts)
    for h in range(8):
        ho[mine, h * 128 : (h + 1) * 128] = (outs[h] / mass[:, h : h + 1]).astype(BF16)

    spread(ho, 14, h1r, h2r, h3r)

    local(wo_hbm, wo, 1).wait()
    own_half = rows(c * 256, 256)
    hpb[own_half, :] = dot(ho[own_half, :], wo[...]).astype(BF16)
    for n in (0, 1):
        wait(ho.at[rows((1 - c) * 256 + n * 128, 128), :], h3r.at[n])
    other_half = rows((1 - c) * 256, 256)
    hpb[other_half, :] = dot(ho[other_half, :], wo[...]).astype(BF16)

    def send_z(k, carry):
        q = lax.rem(z + k, 8)
        zs[q] = dot(place_t[rows(q * 64, 64), :], hpb[...]).astype(BF16)
        send(zs.at[q], zr.at[z], bsem.at[17], zrr.at[z], (c, s, q))
        return carry

    lax.fori_loop(1, 8, send_z, 0)
    total = dot(place_t[rows(z * 64, 64), :], hpb[...])
    for m in range(4):

        @pl.when(z * 4 + m != j)
        def _():
            wait(raw.at[rows(m * 16, 16), :], rawr.at[m])

    total = total + raw[...].astype(F32)
    for k in range(1, 8):
        q = lax.rem(z + 8 - k, 8)
        wait(zr.at[q], zrr.at[q])
        total = total + zr[q].astype(F32)
    attended = total.astype(BF16)
    att_ref[...] = attended
    attended = attended.astype(F32)
    my_z = rows(z * 64, 64)
    feat[j, my_z, :] = (attended * fg_ref[:, rows(j * 256, 256)].astype(F32)).astype(BF16)

    def send_feat_z(k, carry):
        send(feat.at[j, my_z, :], feat.at[j, my_z, :], bsem.at[18], zgr.at[z], (c, s, lax.rem(z + k, 8)))
        return carry

    lax.fori_loop(1, 8, send_feat_z, 0)

    squares = jnp.sum(attended * attended, axis=1, keepdims=True)
    squares = jnp.concatenate([jnp.broadcast_to(squares, (64, 128))] * 2, axis=0).T
    st[j] = squares[0:8]

    def send_squares(k, carry):
        i = lax.rem(j + k, 32)
        send(st.at[j], st.at[j], bsem.at[19], asem.at[1], (lax.div(i, 16), lax.rem(i, 16), z))
        return carry

    local(wv_hbm, wv, 2).wait()

    def multiply(i, first=False):
        def half(n, carry):
            at = rows(n * 256, 256)
            product = dot(feat[i, at, :], wv[rows(i * 256, 256), :])
            if first:
                acc[at, :] = product
            else:
                acc[at, :] += product
            return carry

        lax.fori_loop(0, 2, half, 0)

    def send_block(i, dev):
        send(feat.at[i], feat.at[i], bsem.at[20], ftr.at[i], dev)

    def send_top(i, dev):
        send(feat.at[i, 0:256, :], feat.at[i, 0:256, :], bsem.at[20], ftr.at[i], dev)

    def send_bottom(i, dev):
        send(feat.at[i, 256:512, :], feat.at[i, 256:512, :], bsem.at[20], fbr.at[i], dev)

    def wait_halves(i):
        wait(feat.at[i, 0:256, :], ftr.at[i])
        wait(feat.at[i, 256:512, :], fbr.at[i])

    a_up, a_down, a_far = turn(a, 1), turn(a, 3), turn(a, 2)
    b_up, b_down, b_far = turn(b, 1), turn(b, 3), turn(b, 2)

    def fan(i):
        send_block(i, peer(a_up, b))
        send_block(i, peer(a_down, b))
        send_block(i, sib)

    for k in range(1, 8):
        q = lax.rem(z + 8 - k, 8)
        wait(feat.at[j, rows(q * 64, 64), :], zgr.at[q])
    send_block(j, peer(a, b_up))
    send_block(j, peer(a, b_down))
    fan(j)
    lax.fori_loop(1, 32, send_squares, 0)
    multiply(j, first=True)
    i = blk(a, b_down)
    wait(feat.at[i], ftr.at[i])
    send_top(i, peer(a, b_up))
    fan(i)
    i = blk(a, b_up)
    wait(feat.at[i], ftr.at[i])
    send_bottom(i, peer(a, b_down))
    fan(i)

    wait(st.at[0:31], asem.at[1])
    sum_sq = st[0]
    for n in range(1, 32):
        sum_sq = sum_sq + st[n]
    zt[z] = sum_sq

    def send_sum_sq(k, carry):
        send(zt.at[z], zt.at[z], bsem.at[21], ztr.at[z], (c, s, lax.rem(z + k, 8)))
        return carry

    lax.fori_loop(1, 8, send_sum_sq, 0)

    i = blk(a, b_far)
    wait_halves(i)
    fan(i)

    def b_order(b_, n):
        step = jnp.where(n == 0, 0, jnp.where(n == 1, 3, n - 1))
        return lax.rem(b_ + step, 4)

    def sib_blk(a_, b_):
        return (1 - c) * 16 + seq_of(1 - c, a_, b_)

    def take(i):
        wait(feat.at[i], ftr.at[i])
        multiply(i)

    def near(n, carry):
        bn = b_order(b, n)
        i = blk(a_down, bn)
        wait(feat.at[i], ftr.at[i])
        send_top(i, peer(a_up, b))
        send_block(i, sib)
        k = blk(a_up, bn)
        wait(feat.at[k], ftr.at[k])
        send_bottom(k, peer(a_down, b))
        send_block(k, sib)

        @pl.when(n > 0)
        def _():
            multiply(blk(a, bn))

        take(sib_blk(b, b_order(a, n)))
        return carry

    lax.fori_loop(0, 4, near, 0)

    def far(n, carry):
        bn = b_order(b, n)
        i = blk(a_far, bn)
        wait_halves(i)
        send_block(i, sib)
        multiply(blk(a_down, bn))
        multiply(blk(a_up, bn))
        multiply(i)
        sn = b_order(a, n)
        take(sib_blk(turn(b, 3), sn))
        take(sib_blk(turn(b, 1), sn))
        return carry

    lax.fori_loop(0, 4, far, 0)

    def last(n, carry):
        take(sib_blk(turn(b, 2), b_order(a, n)))
        return carry

    lax.fori_loop(0, 4, last, 0)

    for k in range(1, 8):
        q = lax.rem(z + 8 - k, 8)
        wait(zt.at[q], ztr.at[q])
    entries = acc.shape[1]
    offset = (j * 8 + z) * entries
    entry = (offset + lax.broadcasted_iota(jnp.int32, (1, entries), 1)).astype(F32)
    token = tok_ref[...].astype(F32)
    for g in range(4):
        root = []
        for q in (2 * g, 2 * g + 1):
            root.append(column(lax.rsqrt(zt[q][0:1] * (1.0 / 8192.0) + epsilon))[0:64, 0:1])
        logits = acc[g * 128 : (g + 1) * 128, :] * jnp.concatenate(root, axis=0)
        token_col = column(token[g : g + 1, :])[:, 0:1]
        picked = jnp.sum(jnp.where(entry == token_col, logits, 0.0), axis=1, keepdims=True)
        peak = jnp.max(logits, axis=1, keepdims=True)
        exp_sum = jnp.sum(jnp.exp(logits - peak), axis=1, keepdims=True)
        flat = jnp.where(lane == 0, peak, jnp.where(lane == 1, exp_sum, picked)).T
        for n in range(3):
            fs[j, n * 4 + g : n * 4 + g + 1, :] = flat[n : n + 1]
    fs[j, 12:16, :] = jnp.zeros((4, 128), F32)

    def send_stats(k, carry):
        i = lax.rem(j + k, 32)
        send(fs.at[j], fs.at[j], bsem.at[22], asem.at[2], (lax.div(i, 16), lax.rem(i, 16), z))
        return carry

    lax.fori_loop(1, 32, send_stats, 0)

    def join_stats(ref, count):
        top = ref[0, 0:4, :]
        for n in range(1, count):
            top = jnp.maximum(top, ref[n, 0:4, :])
        exp_total = jnp.zeros((4, 128), F32)
        picked_total = jnp.zeros((4, 128), F32)
        for n in range(count):
            exp_total = exp_total + ref[n, 4:8, :] * jnp.exp(ref[n, 0:4, :] - top)
            picked_total = picked_total + ref[n, 8:12, :]
        return top, exp_total, picked_total

    wait(fs.at[0:31], asem.at[2])
    top, exp_total, picked_total = join_stats(fs, 32)
    fz[z, 0:4, :] = top
    fz[z, 4:8, :] = exp_total
    fz[z, 8:12, :] = picked_total
    fz[z, 12:16, :] = jnp.zeros((4, 128), F32)

    def send_final(k, carry):
        send(fz.at[z], fz.at[z], bsem.at[23], fzr.at[z], (c, s, lax.rem(z + k, 8)))
        return carry

    lax.fori_loop(1, 8, send_final, 0)
    for k in range(1, 8):
        q = lax.rem(z + 8 - k, 8)
        wait(fz.at[q], fzr.at[q])
    top, exp_total, picked_total = join_stats(fz, 8)
    lp_ref[...] = picked_total - top - jnp.log(exp_total)

    wait(xn.at[0:496], bsem.at[0])

    @pl.when(holds_raw)
    def _():
        wait(xn.at[0:496], bsem.at[1])

    wait(r1, bsem.at[2])
    wait(r2.at[0:3], bsem.at[3])
    wait(r3.at[0:3], bsem.at[4])
    for ref, n in ((qkv, 5), (ho, 14)):
        wait(ref.at[0:48], bsem.at[n])
        wait(ref.at[0:192], bsem.at[n + 1])
        wait(ref.at[0:256], bsem.at[n + 2])
    wait(rc1, bsem.at[8])
    wait(rm1, bsem.at[9])
    wait(rc2.at[0:3], bsem.at[10])
    wait(rm2.at[0:3], bsem.at[11])
    wait(rc3.at[0:3], bsem.at[12])
    wait(rm3.at[0:3], bsem.at[13])
    wait(zr.at[0:7], bsem.at[17])
    wait(zr.at[0:7], bsem.at[18])
    wait(st.at[0:31], bsem.at[19])
    wait(feat.at[0:31], bsem.at[20])
    wait(zt.at[0:7], bsem.at[21])
    wait(fs.at[0:31], bsem.at[22])
    wait(fz.at[0:7], bsem.at[23])


def rope_tables(cache_len):
    side = lax.axis_index("side")
    seq = lax.axis_index("seq")
    along, across = seq // 4, seq % 4
    a = along + side * (across - along)
    b = across + side * (along - across)
    row0 = side * 256 + a * 64 + b * 16
    half_dim = HD // 2
    mine = jnp.sum(jnp.where(jnp.arange(TRAJ) == row0 // 128, cache_len, 0))
    places = mine + row0 % 128 + jnp.arange(16, dtype=jnp.int32)
    spread = jnp.exp(
        jnp.arange(half_dim).astype(F32) * (-2.0 * math.log(rope_base) / HD)
    )
    angles = places.astype(F32)[:, None] * spread[None, :]
    cosine = jnp.cos(angles)
    sine = jnp.sin(angles)
    return (
        jnp.concatenate([cosine, cosine], axis=1),
        jnp.concatenate([-sine, sine], axis=1),
    )


def per_device(
    x_rows,
    attn_gain,
    final_gain,
    w_query,
    w_kv,
    w_out,
    kv_cache,
    w_vocab,
    token_ids,
    cache_len,
    row_traj,
):
    cosine, sine = rope_tables(cache_len)
    entries = w_vocab.shape[1]
    vmem = pl.BlockSpec(memory_space=pltpu.VMEM)
    smem = pl.BlockSpec(memory_space=pltpu.SMEM)
    hbm = pl.BlockSpec(memory_space=pl.ANY)
    dma = pltpu.SemaphoreType.DMA
    attended, logprob = pl.pallas_call(
        kernel,
        out_shape=(
            jax.ShapeDtypeStruct((64, 256), BF16),
            jax.ShapeDtypeStruct((4, 128), F32),
        ),
        in_specs=[vmem, vmem, vmem, vmem, vmem, hbm, hbm, hbm, vmem, smem, vmem, vmem, vmem],
        out_specs=(vmem, vmem),
        scratch_shapes=[
            pltpu.VMEM((1024, 256), BF16),
            pltpu.VMEM((2, 4, 1024, 128), BF16),
            pltpu.VMEM((8192, entries), BF16),
            pltpu.VMEM((16, 8192), BF16),
            pltpu.VMEM((512, 256), BF16),
            pltpu.VMEM((64, 256), BF16),
            pltpu.VMEM((512, 512), BF16),
            pltpu.VMEM((512, 512), BF16),
            pltpu.VMEM((512, 256), BF16),
            pltpu.VMEM((512, 1280), F32),
            pltpu.VMEM((256, 1280), F32),
            pltpu.VMEM((4, 64, 1280), BF16),
            pltpu.VMEM((4, 64, 1280), BF16),
            pltpu.VMEM((64, 1280), F32),
            pltpu.VMEM((4, 16, 1280), F32),
            pltpu.VMEM((512, 1280), BF16),
            pltpu.VMEM((512, 1024), F32),
            pltpu.VMEM((2, 512, 128), F32),
            pltpu.VMEM((256, 1024), F32),
            pltpu.VMEM((2, 256, 128), F32),
            pltpu.VMEM((4, 64, 1024), BF16),
            pltpu.VMEM((4, 2, 64, 128), F32),
            pltpu.VMEM((4, 64, 1024), BF16),
            pltpu.VMEM((4, 2, 64, 128), F32),
            pltpu.VMEM((64, 1024), F32),
            pltpu.VMEM((2, 64, 128), F32),
            pltpu.VMEM((4, 16, 1024), F32),
            pltpu.VMEM((4, 2, 16, 128), F32),
            pltpu.VMEM((512, 1024), BF16),
            pltpu.VMEM((512, 256), BF16),
            pltpu.VMEM((8, 64, 256), BF16),
            pltpu.VMEM((8, 64, 256), BF16),
            pltpu.VMEM((32, 512, 256), BF16),
            pltpu.VMEM((512, entries), F32),
            pltpu.VMEM((32, 8, 128), F32),
            pltpu.VMEM((8, 8, 128), F32),
            pltpu.VMEM((32, 16, 128), F32),
            pltpu.VMEM((8, 16, 128), F32),
            dma((3,)),
            dma((24,)),
            dma((3,)),
            dma((4,)),
            dma((4,)),
            dma((4,)),
            dma((4,)),
            dma((4,)),
            dma((4,)),
            dma((2,)),
            dma((4,)),
            dma((8,)),
            dma((8,)),
            dma((4,)),
            dma((4,)),
            dma((2,)),
            dma((8,)),
            dma((8,)),
            dma((32,)),
            dma((32,)),
            dma((8,)),
            dma((8,)),
        ],
        compiler_params=pltpu.CompilerParams(
            collective_id=0, has_side_effects=True, vmem_limit_bytes=60 * 1024 * 1024
        ),
        cost_estimate=pl.CostEstimate(
            flops=8_000_000_000, bytes_accessed=14_000_000, transcendentals=5_000_000
        ),
    )(
        x_rows,
        attn_gain.reshape(1, -1),
        final_gain.reshape(1, -1),
        w_query,
        w_kv.reshape(w_kv.shape[0], -1),
        w_out,
        kv_cache,
        w_vocab,
        token_ids.reshape(4, 128),
        cache_len,
        row_traj.reshape(4, 128),
        cosine,
        sine,
    )
    return attended, logprob.reshape(-1)


def solution(mesh):
    in_specs = (
        P(("side", "seq"), None),
        P(),
        P(),
        P(("side", "seq"), "tensor"),
        P(("side", "seq"), None, "tensor"),
        P("tensor", ("side", "seq")),
        P(None, None, ("side", "seq"), "tensor"),
        P(None, ("side", "seq", "tensor")),
        P(),
        P(),
        P(),
    )
    out_specs = (P("tensor", ("side", "seq")), P())
    return jax.shard_map(
        per_device, mesh=mesh, in_specs=in_specs, out_specs=out_specs, check_vma=False
    )
```

```python
import functools
import math

import jax
import jax.numpy as jnp
import numpy as np
from jax import lax
from jax.experimental import pallas as pl
from jax.experimental.pallas import tpu as pltpu
from jax.sharding import PartitionSpec as P

HD = 128
TRAJ = 4
MESH = pl.DeviceIdType.MESH

epsilon = 1e-06
rope_base = 1000000.0
masked_low = -1e30
SCALE2 = float(HD) ** (-0.5) * math.log2(math.e)

F32 = jnp.float32
BF16 = jnp.bfloat16


def dot(a, b):
    return jnp.dot(a, b, preferred_element_type=F32)


def dot_nt(a, b):
    return lax.dot_general(a, b, (((1,), (1,)), ((), ())), preferred_element_type=F32)


def rows(start, size):
    return pl.ds(pl.multiple_of(start, size), size)


def span(start, size, unit):
    return pl.ds(pl.multiple_of(start, unit), size)


def column(row):
    return jnp.broadcast_to(row, (128, 128)).T


def merge(parts):
    top = functools.reduce(jnp.maximum, [p[1] for p in parts])
    factors = [jnp.exp2((p[1] - top) * SCALE2) for p in parts]
    mass = sum(p[2] * f for p, f in zip(parts, factors))
    outs = [
        sum(p[0](h) * f[:, h : h + 1] for p, f in zip(parts, factors)) for h in range(8)
    ]
    return outs, top, mass


def kernel(
    x_ref,
    ag_ref,
    fg_ref,
    wq_hbm,
    wkv_ref,
    wo_hbm,
    kv_hbm,
    wv_hbm,
    tok_ref,
    clen_ref,
    traj_ref,
    spread_ref,
    att_ref,
    lp_ref,
    wq,
    wo,
    keys,
    values,
    wv,
    nx,
    xn,
    raw,
    place,
    place_t,
    xs,
    part,
    r1,
    s2,
    r2,
    sum2,
    r3,
    qkv,
    o_all,
    ml_all,
    rc1,
    rm1,
    sc2,
    sm2,
    rc2,
    rm2,
    oc2,
    mc2,
    rc3,
    rm3,
    ho,
    hpb,
    zs,
    zr,
    feat,
    tail,
    acc,
    flat,
    st,
    zt,
    fs,
    fz,
    lsem,
    bsem,
    asem,
    rawr,
    p1r,
    p2r,
    p3r,
    g1r,
    g2r,
    g3r,
    c1r,
    c2r,
    c3r,
    h1r,
    h2r,
    h3r,
    zrr,
    zgr,
    ftr,
    fbr,
    qbr,
    qar,
    qur,
    qdr,
    qsr,
    ztr,
    fzr,
):
    c = lax.axis_index("side")
    s = lax.axis_index("seq")
    z = lax.axis_index("tensor")
    j = c * 16 + s
    along = lax.div(s, 4)
    across = lax.rem(s, 4)
    a = along + c * (across - along)
    b = across + c * (along - across)
    row0 = c * 256 + a * 64 + b * 16

    def seq_of(side, a_, b_):
        straight = a_ * 4 + b_
        return straight + side * (b_ * 4 + a_ - straight)

    def peer(a_, b_):
        return (c, seq_of(c, a_, b_), z)

    def turn(v, k):
        return lax.rem(v + k, 4)

    sib = (1 - c, s, z)

    def send(src, dst, ssem, rsem, dev):
        pltpu.make_async_remote_copy(
            src_ref=src, dst_ref=dst, send_sem=ssem, recv_sem=rsem, device_id=dev, device_id_type=MESH
        ).start()

    def wait(ref, sem):
        pltpu.make_async_copy(ref, ref, sem).wait()

    def local(src, dst, n):
        return pltpu.make_async_copy(src, dst, lsem.at[n])

    copies = [
        local(wq_hbm, wq, 0),
        local(kv_hbm.at[0], keys.at[:, :, 0:128], 1),
        local(kv_hbm.at[1], values.at[:, :, 0:128], 2),
        local(wo_hbm, wo, 3),
        local(wv_hbm, wv, 4),
    ]
    for copy in copies:
        copy.start()

    barrier = pltpu.get_barrier_semaphore()

    def greet(k, carry):
        i = lax.rem(j + k, 32)
        pl.semaphore_signal(barrier, inc=1, device_id=(lax.div(i, 16), lax.rem(i, 16), z), device_id_type=MESH)
        return carry

    lax.fori_loop(1, 32, greet, 0)

    def greet_z(k, carry):
        pl.semaphore_signal(barrier, inc=1, device_id=(c, s, lax.rem(z + k, 8)), device_id_type=MESH)
        return carry

    lax.fori_loop(1, 8, greet_z, 0)

    total = jnp.zeros((16, 1), F32)
    for n in range(8):
        v = x_ref[:, n * 1024 : (n + 1) * 1024].astype(F32)
        total = total + jnp.sum(v * v, axis=1, keepdims=True)
    unit = lax.rsqrt(total * (1.0 / 8192.0) + epsilon)
    for n in range(64):
        cols = slice(n * 128, (n + 1) * 128)
        v = x_ref[:, cols].astype(F32)
        nx[:, cols] = (v * unit * ag_ref[n : n + 1, :].astype(F32)).astype(BF16)

    pl.semaphore_wait(barrier, 38)

    def send_rows(k, carry):
        i = lax.rem(j + k, 32)
        send(
            nx.at[:, rows(i * 256, 256)],
            xn.at[rows(j * 16, 16), :],
            bsem.at[0],
            asem.at[0],
            (lax.div(i, 16), lax.rem(i, 16), z),
        )
        return carry

    lax.fori_loop(1, 32, send_rows, 0)
    xn[rows(j * 16, 16), :] = nx[:, rows(j * 256, 256)]

    quarter = lax.rem(j, 4)
    holds_raw = lax.div(j, 4) == z

    @pl.when(holds_raw)
    def _():
        def send_raw(k, carry):
            i = lax.rem(j + k, 32)
            send(
                x_ref.at[:, rows(i * 256, 256)],
                raw.at[rows(quarter * 16, 16), :],
                bsem.at[1],
                rawr.at[quarter],
                (lax.div(i, 16), lax.rem(i, 16), z),
            )
            return carry

        lax.fori_loop(1, 32, send_raw, 0)
        raw[rows(quarter * 16, 16), :] = x_ref[:, rows(j * 256, 256)]

    traj = traj_ref[...].astype(F32)
    traj_cols = [column(traj[g : g + 1, :]) for g in range(4)]
    sub = lax.broadcasted_iota(jnp.int32, (128, 128), 0)
    lane = lax.broadcasted_iota(jnp.int32, (128, 128), 1)
    for g in range(4):
        step_col = jnp.zeros((128, 1), F32)
        step_row = jnp.zeros((1, 128), F32)
        for e in range(g + 1):
            same = jnp.where(traj_cols[g] == traj[e : e + 1, :], 1.0, 0.0)
            if e == g:
                same = jnp.where(lane < sub, same, 0.0)
            step_col = step_col + jnp.sum(same, axis=1, keepdims=True)
            same = jnp.where(traj_cols[e] == traj[g : g + 1, :], 1.0, 0.0)
            if e == g:
                same = jnp.where(sub < lane, same, 0.0)
            step_row = step_row + jnp.sum(same, axis=0, keepdims=True)
        slot_col = traj_cols[g] * 128.0 + step_col
        slot_row = traj[g : g + 1, :] * 128.0 + step_row
        for e in range(4):
            place_t[g * 128 : (g + 1) * 128, e * 128 : (e + 1) * 128] = jnp.where(
                (lane + e * 128).astype(F32) == slot_col, 1.0, 0.0
            ).astype(BF16)
            place[e * 128 : (e + 1) * 128, g * 128 : (g + 1) * 128] = jnp.where(
                (sub + e * 128).astype(F32) == slot_row, 1.0, 0.0
            ).astype(BF16)

    key_place = j * 1024 + lax.broadcasted_iota(jnp.int32, (1024, 128), 0)
    first_lane = lax.broadcasted_iota(jnp.int32, (1024, 128), 1) == 0
    for t in range(4):
        past = jnp.logical_and(first_lane, key_place >= clen_ref[t])
        keys[t, :, 128:256] = jnp.where(past, masked_low, 0.0).astype(BF16)
        values[t, :, 128:256] = jnp.ones((1024, 128), BF16)
    acc[...] = jnp.zeros(acc.shape, F32)

    own_traj = lax.div(row0, 128)
    own_step = lax.rem(row0, 128)
    cached = clen_ref[0]
    for t in range(1, 4):
        cached = jnp.where(own_traj == t, clen_ref[t], cached)
    lane16 = lane[0:16]
    angles = (cached + own_step + sub[0:16]).astype(F32) * spread_ref[...]
    cosine = jnp.cos(angles)
    sine = jnp.sin(angles)
    sine = jnp.where(lane16 < 64, -sine, sine)

    copies[0].wait()
    wait(xn.at[0:496], asem.at[0])

    def project(half):
        at = rows(half * 256, 256)
        xs[at, :] = dot(place[at, :], xn[...]).astype(BF16)
        part[at, 0:1024] = dot(xs[at, :], wq[...])
        part[at, 1024:1152] = dot(xs[at, :], wkv_ref[:, 0, :])
        part[at, 1152:1280] = dot(xs[at, :], wkv_ref[:, 1, :])

    project(1 - c)
    for k in (1, 2, 3, 0):
        q = turn(b, k)
        send(part.at[rows((1 - c) * 256 + q * 64, 64), :], r1.at[rows(q * 64, 64), :], bsem.at[2], p1r.at[q], sib)
    project(c)

    def pair_sum(q):
        wait(r1.at[rows(q * 64, 64), :], p1r.at[q])
        return part[rows(c * 256 + q * 64, 64), :] + r1[rows(q * 64, 64), :]

    for k in (1, 2, 3):
        q = turn(a, k)
        s2[q] = pair_sum(q).astype(BF16)
        send(s2.at[q], r2.at[a], bsem.at[3], p2r.at[a], peer(q, b))
    sum2[...] = pair_sum(a)
    for k in (3, 2, 1):
        q = turn(a, k)
        wait(r2.at[q], p2r.at[q])
        sum2[...] += r2[q].astype(F32)
    for k in (1, 2, 3):
        q = turn(b, k)
        send(sum2.at[rows(q * 16, 16), :], r3.at[b], bsem.at[4], p3r.at[b], peer(a, q))
    r3[b] = sum2[rows(b * 16, 16), :]
    for k in (3, 2, 1):
        q = turn(b, k)
        wait(r3.at[q], p3r.at[q])
    sums = (r3[0] + r3[1]) + (r3[2] + r3[3])
    mine = rows(row0, 16)
    for h in range(9):
        v = sums[:, h * 128 : (h + 1) * 128]
        qkv[mine, h * 128 : (h + 1) * 128] = (v * cosine + pltpu.roll(v, 64, 1) * sine).astype(BF16)
    qkv[mine, 1152:1280] = sums[:, 1152:1280].astype(BF16)

    def spread(ref, n, r_b, r_a, r_s):
        for k in (1, 2, 3):
            send(ref.at[mine, :], ref.at[mine, :], bsem.at[n], r_b.at[b], peer(a, turn(b, k)))
        for k in (3, 2, 1):
            q = turn(b, k)
            wait(ref.at[rows(c * 256 + a * 64 + q * 16, 16), :], r_b.at[q])
        at = rows(c * 256 + a * 64, 64)
        for k in (1, 2, 3):
            send(ref.at[at, :], ref.at[at, :], bsem.at[n + 1], r_a.at[a], peer(turn(a, k), b))
        for k in (3, 2, 1):
            q = turn(a, k)
            wait(ref.at[rows(c * 256 + q * 64, 64), :], r_a.at[q])
        for n_half in (0, 1):
            at = rows(c * 256 + n_half * 128, 128)
            send(ref.at[at, :], ref.at[at, :], bsem.at[n + 2], r_s.at[n_half], sib)

    spread(qkv, 5, g1r, g2r, g3r)

    copies[1].wait()
    copies[2].wait()
    one = jnp.where(lax.broadcasted_iota(jnp.int32, (512, 128), 1) == 0, 1.0, 0.0).astype(BF16)

    def attend(t):
        at = rows(t * 128, 128)
        peaks = jnp.zeros((128, 128), F32)
        masses = jnp.zeros((128, 128), F32)
        for h in range(0, 8, 4):
            heads = jnp.concatenate(
                [qkv[at, (h + e) * 128 : (h + e + 1) * 128] for e in range(4)], axis=0
            )
            scores = dot_nt(jnp.concatenate([heads, one], axis=1), keys[t])
            peak = jnp.max(scores, axis=1, keepdims=True)
            weights = jnp.exp2((scores - peak) * SCALE2).astype(BF16)
            out = dot(weights, values[t])
            for e in range(4):
                part_rows = slice(e * 128, (e + 1) * 128)
                o_all[at, (h + e) * 128 : (h + e + 1) * 128] = out[part_rows, 0:128]
                peaks = jnp.where(lane == h + e, peak[part_rows], peaks)
                masses = jnp.where(lane == h + e, out[part_rows, 128:256], masses)
        ml_all[0, at, :] = peaks
        ml_all[1, at, :] = masses

    def attend_other(n, carry):
        t = (1 - c) * 2 + n
        at = rows(t * 128, 128)
        wait(qkv.at[at, :], g3r.at[n])
        attend(t)
        to = rows(n * 128, 128)
        send(o_all.at[at, :], rc1.at[to, :], bsem.at[8], c1r.at[n], sib)
        send(ml_all.at[:, at, :], rm1.at[:, to, :], bsem.at[9], c1r.at[n + 2], sib)
        return carry

    def join_pair(q):
        at = rows(c * 256 + q * 64, 64)
        to = slice(q * 64, (q + 1) * 64)
        outs, top, mass = merge(
            [
                (lambda h: o_all[at, h * 128 : (h + 1) * 128], ml_all[0, at, :], ml_all[1, at, :]),
                (lambda h: rc1[to, h * 128 : (h + 1) * 128], rm1[0, to, :], rm1[1, to, :]),
            ]
        )

        @pl.when(q != a)
        def _():
            for h in range(8):
                sc2[q, :, h * 128 : (h + 1) * 128] = outs[h].astype(BF16)
            sm2[q, 0] = top
            sm2[q, 1] = mass
            send(sc2.at[q], rc2.at[a], bsem.at[10], c2r.at[a], peer(q, b))
            send(sm2.at[q], rm2.at[a], bsem.at[11], c2r.at[a + 4], peer(q, b))

        @pl.when(q == a)
        def _():
            for h in range(8):
                oc2[:, h * 128 : (h + 1) * 128] = outs[h]
            mc2[0] = top
            mc2[1] = mass

    attend(c * 2)
    lax.fori_loop(0, 2, attend_other, 0)
    wait(rc1.at[0:128, :], c1r.at[0])
    wait(rm1.at[:, 0:128, :], c1r.at[2])
    join_pair(0)
    join_pair(1)
    attend(c * 2 + 1)
    wait(rc1.at[128:256, :], c1r.at[1])
    wait(rm1.at[:, 128:256, :], c1r.at[3])
    join_pair(2)
    join_pair(3)

    own_rows = rows(own_traj * 128, 128)
    own_q = jnp.concatenate([qkv[mine, h * 128 : (h + 1) * 128] for h in range(8)], axis=0)
    own_scores = dot_nt(own_q, qkv[own_rows, 1024:1152])
    own_scores = jnp.where(lane <= own_step + (sub & 15), own_scores, masked_low)
    own_peak = jnp.max(own_scores, axis=1, keepdims=True)
    own_weights = jnp.exp2((own_scores - own_peak) * SCALE2)
    own_mass = jnp.sum(own_weights, axis=1, keepdims=True)
    own_out = dot(own_weights.astype(BF16), qkv[own_rows, 1152:1280])
    own_peaks = jnp.zeros((16, 128), F32)
    own_masses = jnp.zeros((16, 128), F32)
    for h in range(8):
        own_peaks = jnp.where(lane16 == h, own_peak[h * 16 : (h + 1) * 16], own_peaks)
        own_masses = jnp.where(lane16 == h, own_mass[h * 16 : (h + 1) * 16], own_masses)

    def arrived(k):
        q = turn(a, k)
        wait(rc2.at[q], c2r.at[q])
        wait(rm2.at[q], c2r.at[q + 4])
        return (lambda h: rc2[q, :, h * 128 : (h + 1) * 128].astype(F32), rm2[q, 0], rm2[q, 1])

    parts = [(lambda h: oc2[:, h * 128 : (h + 1) * 128], mc2[0], mc2[1])]
    parts += [arrived(k) for k in (3, 2, 1)]
    outs, top, mass = merge(parts)
    for h in range(8):
        oc2[:, h * 128 : (h + 1) * 128] = outs[h]
    mc2[0] = top
    mc2[1] = mass
    for k in (1, 2, 3):
        q = turn(b, k)
        send(oc2.at[rows(q * 16, 16), :], rc3.at[b], bsem.at[12], c3r.at[b], peer(a, q))
        send(mc2.at[:, rows(q * 16, 16), :], rm3.at[b], bsem.at[13], c3r.at[b + 4], peer(a, q))
    rc3[b] = oc2[rows(b * 16, 16), :]
    rm3[b] = mc2[:, rows(b * 16, 16), :]
    for k in (3, 2, 1):
        q = turn(b, k)
        wait(rc3.at[q], c3r.at[q])
        wait(rm3.at[q], c3r.at[q + 4])
    parts = [(lambda h, q=q: rc3[q, :, h * 128 : (h + 1) * 128], rm3[q, 0], rm3[q, 1]) for q in range(4)]
    parts.append((lambda h: own_out[h * 16 : (h + 1) * 16], own_peaks, own_masses))
    outs, top, mass = merge(parts)
    for h in range(8):
        ho[mine, h * 128 : (h + 1) * 128] = (outs[h] / mass[:, h : h + 1]).astype(BF16)

    spread(ho, 14, h1r, h2r, h3r)

    copies[3].wait()
    own_half = rows(c * 256, 256)
    hpb[own_half, :] = dot(ho[own_half, :], wo[...]).astype(BF16)
    for n in (0, 1):
        wait(ho.at[rows((1 - c) * 256 + n * 128, 128), :], h3r.at[n])
    other_half = rows((1 - c) * 256, 256)
    hpb[other_half, :] = dot(ho[other_half, :], wo[...]).astype(BF16)

    zs[...] = dot(place_t[...], hpb[...]).astype(BF16)

    def send_z_tail(k, carry):
        q = lax.rem(z + k, 8)
        send(zs.at[span(q * 64 + 48, 16, 16), :], zr.at[z, 48:64, :], bsem.at[17], zrr.at[z], (c, s, q))
        return carry

    def send_z_head(k, carry):
        q = lax.rem(z + k, 8)
        send(zs.at[span(q * 64, 48, 16), :], zr.at[z, 0:48, :], bsem.at[18], zrr.at[z + 8], (c, s, q))
        return carry

    lax.fori_loop(1, 8, send_z_tail, 0)
    lax.fori_loop(1, 8, send_z_head, 0)
    total = dot(place_t[rows(z * 64, 64), :], hpb[...])
    for m in range(4):

        @pl.when(z * 4 + m != j)
        def _():
            wait(raw.at[rows(m * 16, 16), :], rawr.at[m])

    total = total + raw[...].astype(F32)
    gains = fg_ref[...].astype(F32)
    gain_row = lax.broadcasted_iota(jnp.int32, (64, 128), 0)
    gain = jnp.concatenate(
        [jnp.sum(jnp.where(gain_row == 2 * j + n, gains, 0.0), axis=0, keepdims=True) for n in (0, 1)],
        axis=1,
    )

    def block_of(a_, b_):
        return c * 16 + a_ * 4 + b_

    here = block_of(a, b)
    tail_z = rows(z * 16, 16)
    head_z = span(z * 48, 48, 16)
    a_up, a_down, a_far = turn(a, 1), turn(a, 3), turn(a, 2)
    b_up, b_down, b_far = turn(b, 1), turn(b, 3), turn(b, 2)
    z_up = (c, s, lax.rem(z + 1, 8))
    z_down = (c, s, lax.rem(z + 7, 8))

    attended = total[48:64]
    for k in range(1, 8):
        q = lax.rem(z + 8 - k, 8)
        wait(zr.at[q, 48:64, :], zrr.at[q])
        attended = attended + zr[q, 48:64, :].astype(F32)
    attended = attended.astype(BF16)
    att_ref[48:64, :] = attended
    tail[here, tail_z, :] = (attended.astype(F32) * gain).astype(BF16)
    for k in (1, 2, 3):
        ref = tail.at[here, tail_z, :]
        send(ref, ref, bsem.at[19], qbr.at[b], peer(a, turn(b, k)))

    attended = total[0:48]
    for k in range(1, 8):
        q = lax.rem(z + 8 - k, 8)
        wait(zr.at[q, 0:48, :], zrr.at[q + 8])
        attended = attended + zr[q, 0:48, :].astype(F32)
    attended = attended.astype(BF16)
    att_ref[0:48, :] = attended
    feat[here, head_z, :] = (attended.astype(F32) * gain).astype(BF16)

    def send_feat_z(k, carry):
        ref = feat.at[here, head_z, :]
        send(ref, ref, bsem.at[20], zgr.at[z], (c, s, lax.rem(z + k, 8)))
        return carry

    lax.fori_loop(1, 8, send_feat_z, 0)

    def send_chunk(q):
        chunk = feat.at[here, span(q * 48, 48, 16), :]
        for dev in (peer(a_up, b), peer(a_down, b), peer(a, b_up), peer(a, b_down), sib):
            send(chunk, chunk, bsem.at[21], ftr.at[here], dev)

    def pass_chunk(k, carry):
        q = lax.rem(z + jnp.where(lax.rem(k, 2) == 1, lax.div(k + 1, 2), 8 - lax.div(k, 2)), 8)
        wait(feat.at[here, span(q * 48, 48, 16), :], zgr.at[q])
        send_chunk(q)
        return carry

    send_chunk(z)

    for k in (3, 2, 1):
        q = turn(b, k)
        wait(tail.at[block_of(a, q), tail_z, :], qbr.at[q])
    for k in (1, 2, 3):
        ref = tail.at[pl.ds(block_of(a, 0), 4), tail_z, :]
        send(ref, ref, bsem.at[22], qar.at[a], peer(turn(a, k), b))

    squares = att_ref[...].astype(F32)
    squares = jnp.sum(squares * squares, axis=1, keepdims=True)
    squares = jnp.concatenate([jnp.broadcast_to(squares, (64, 128))] * 2, axis=0).T
    st[j] = squares[0:8]

    def send_squares(k, carry):
        i = lax.rem(j + k, 32)
        send(st.at[j], st.at[j], bsem.at[23], asem.at[1], (lax.div(i, 16), lax.rem(i, 16), z))
        return carry

    lax.fori_loop(1, 3, pass_chunk, 0)

    def tail_of(q):
        return tail.at[pl.ds(c * 16, 16), rows(q * 16, 16), :]

    for k in (3, 2, 1):
        q = turn(a, k)
        wait(tail.at[pl.ds(block_of(q, 0), 4), tail_z, :], qar.at[q])
    send(tail_of(z), tail_of(z), bsem.at[24], qur.at[1], z_up)
    send(tail_of(z), tail_of(z), bsem.at[24], qdr.at[1], z_down)
    send(tail_of(z), tail_of(z), bsem.at[24], qsr.at[z], sib)

    lax.fori_loop(3, 8, pass_chunk, 0)
    lax.fori_loop(1, 32, send_squares, 0)
    copies[4].wait()

    def multiply(*blocks):
        acc[0:384, :] += sum(
            dot_nt(feat[side * 16 + a_ * 4 + b_], wv[:, rows(side * 4096 + seq_of(side, a_, b_) * 256, 256)])
            for side, a_, b_ in blocks
        )

    def send_block(i, dev):
        send(feat.at[i], feat.at[i], bsem.at[21], ftr.at[i], dev)

    def send_top(i, dev):
        ref = feat.at[i, 0:192, :]
        send(ref, ref, bsem.at[21], ftr.at[i], dev)

    def send_bottom(i, dev):
        ref = feat.at[i, 192:384, :]
        send(ref, ref, bsem.at[21], fbr.at[i], dev)

    def wait_block(i):
        wait(feat.at[i], ftr.at[i])

    def wait_halves(i):
        wait(feat.at[i, 0:192, :], ftr.at[i])
        wait(feat.at[i, 192:384, :], fbr.at[i])

    def fan(i):
        send_block(i, peer(a_up, b))
        send_block(i, peer(a_down, b))
        send_block(i, sib)

    i = block_of(a, b_down)
    wait_block(i)
    send_top(i, peer(a, b_up))
    fan(i)
    i = block_of(a, b_up)
    wait_block(i)
    send_bottom(i, peer(a, b_down))
    fan(i)

    wait(st.at[0:31], asem.at[1])
    sum_sq = st[0]
    for n in range(1, 32):
        sum_sq = sum_sq + st[n]
    zt[z] = sum_sq

    def send_sum_sq(k, carry):
        send(zt.at[z], zt.at[z], bsem.at[25], ztr.at[z], (c, s, lax.rem(z + k, 8)))
        return carry

    lax.fori_loop(1, 8, send_sum_sq, 0)

    i = block_of(a, b_far)
    wait_halves(i)
    fan(i)

    def order(b_, n):
        step = jnp.where(n == 0, 0, jnp.where(n == 1, 3, n - 1))
        return lax.rem(b_ + step, 4)

    def from_sib(a_, b_):
        wait_block((1 - c) * 16 + a_ * 4 + b_)
        return (1 - c, a_, b_)

    def near(n, carry):
        bn = order(b, n)
        i = block_of(a_down, bn)
        wait_block(i)
        send_top(i, peer(a_up, b))
        send_block(i, sib)
        i = block_of(a_up, bn)
        wait_block(i)
        send_bottom(i, peer(a_down, b))
        send_block(i, sib)

        q = lax.rem(z + 7 - n, 8)
        wait(tail_of(q), qur.at[n + 1])
        send(tail_of(q), tail_of(q), bsem.at[24], qsr.at[q], sib)

        @pl.when(n < 3)
        def _():
            send(tail_of(q), tail_of(q), bsem.at[24], qur.at[n + 2], z_up)
            p = lax.rem(z + 1 + n, 8)
            wait(tail_of(p), qdr.at[n + 1])
            send(tail_of(p), tail_of(p), bsem.at[24], qsr.at[p], sib)

            @pl.when(n < 2)
            def _():
                send(tail_of(p), tail_of(p), bsem.at[24], qdr.at[n + 2], z_down)

        multiply((c, a, bn), (c, a_down, bn), (c, a_up, bn), from_sib(b, order(a, n)))
        return carry

    lax.fori_loop(0, 4, near, 0)

    def far(n, carry):
        bn = order(b, n)
        i = block_of(a_far, bn)
        wait_halves(i)
        send_block(i, sib)
        sn = order(a, n)
        multiply((c, a_far, bn), from_sib(b_down, sn), from_sib(b_up, sn))
        return carry

    lax.fori_loop(0, 4, far, 0)

    for n in range(8):
        wait(tail.at[pl.ds((1 - c) * 16, 16), n * 16 : (n + 1) * 16, :], qsr.at[n])

    def multiply_tail(n, carry):
        side = lax.div(n, 4)
        a_ = lax.rem(n, 4)
        acc[384:512, :] += sum(
            dot_nt(tail[n * 4 + b_], wv[:, rows(side * 4096 + seq_of(side, a_, b_) * 256, 256)])
            for b_ in range(4)
        )
        return carry

    lax.fori_loop(0, 8, multiply_tail, 0)

    def last(n, carry):
        multiply(*[from_sib(b_far, order(a, 2 * n + e)) for e in (0, 1)])
        return carry

    lax.fori_loop(0, 2, last, 0)

    for k in range(1, 8):
        q = lax.rem(z + 8 - k, 8)
        wait(zt.at[q], ztr.at[q])
    entries = acc.shape[1]
    offset = (j * 8 + z) * entries
    entry = (offset + lax.broadcasted_iota(jnp.int32, (1, entries), 1)).astype(F32)
    token = tok_ref[...].astype(F32)
    roots = [column(lax.rsqrt(zt[q][0:1] * (1.0 / 8192.0) + epsilon))[0:64] for q in range(8)]
    token_cols = [column(token[g : g + 1, :]) for g in range(4)]
    tokens = [token_cols[q // 2][(q % 2) * 64 : (q % 2) * 64 + 64] for q in range(8)]

    def regroup(cols):
        return jnp.concatenate([v[0:48] for v in cols] + [v[48:64] for v in cols], axis=0)

    roots = regroup(roots)
    tokens = regroup(tokens)
    for g in range(4):
        at = slice(g * 128, (g + 1) * 128)
        logits = acc[at, :] * roots[at, 0:1]
        picked = jnp.sum(jnp.where(entry == tokens[at, 0:1], logits, 0.0), axis=1, keepdims=True)
        peak = jnp.max(logits, axis=1, keepdims=True)
        exp_sum = jnp.sum(jnp.exp(logits - peak), axis=1, keepdims=True)
        flat[at, :] = jnp.where(lane == 0, peak, jnp.where(lane == 1, exp_sum, picked))
    for g in range(4):
        pieces = []
        for q in (2 * g, 2 * g + 1):
            pieces += [flat[q * 48 : (q + 1) * 48, :], flat[384 + q * 16 : 400 + q * 16, :]]
        stats = jnp.concatenate(pieces, axis=0).T
        for n in range(3):
            fs[j, n * 4 + g : n * 4 + g + 1, :] = stats[n : n + 1]
    fs[j, 12:16, :] = jnp.zeros((4, 128), F32)

    def send_stats(k, carry):
        i = lax.rem(j + k, 32)
        send(fs.at[j], fs.at[j], bsem.at[26], asem.at[2], (lax.div(i, 16), lax.rem(i, 16), z))
        return carry

    lax.fori_loop(1, 32, send_stats, 0)

    def join_stats(ref, count):
        top = ref[0, 0:4, :]
        for n in range(1, count):
            top = jnp.maximum(top, ref[n, 0:4, :])
        exp_total = jnp.zeros((4, 128), F32)
        picked_total = jnp.zeros((4, 128), F32)
        for n in range(count):
            exp_total = exp_total + ref[n, 4:8, :] * jnp.exp(ref[n, 0:4, :] - top)
            picked_total = picked_total + ref[n, 8:12, :]
        return top, exp_total, picked_total

    wait(fs.at[0:31], asem.at[2])
    top, exp_total, picked_total = join_stats(fs, 32)
    fz[z, 0:4, :] = top
    fz[z, 4:8, :] = exp_total
    fz[z, 8:12, :] = picked_total
    fz[z, 12:16, :] = jnp.zeros((4, 128), F32)

    def send_final(k, carry):
        send(fz.at[z], fz.at[z], bsem.at[27], fzr.at[z], (c, s, lax.rem(z + k, 8)))
        return carry

    lax.fori_loop(1, 8, send_final, 0)
    for k in range(1, 8):
        q = lax.rem(z + 8 - k, 8)
        wait(fz.at[q], fzr.at[q])
    top, exp_total, picked_total = join_stats(fz, 8)
    lp_ref[...] = picked_total - top - jnp.log(exp_total)

    wait(xn.at[0:496], bsem.at[0])

    @pl.when(holds_raw)
    def _():
        wait(xn.at[0:496], bsem.at[1])

    wait(r1, bsem.at[2])
    wait(r2.at[0:3], bsem.at[3])
    wait(r3.at[0:3], bsem.at[4])
    for ref, n in ((qkv, 5), (ho, 14)):
        wait(ref.at[0:48], bsem.at[n])
        wait(ref.at[0:192], bsem.at[n + 1])
        wait(ref.at[0:256], bsem.at[n + 2])
    wait(rc1, bsem.at[8])
    wait(rm1, bsem.at[9])
    wait(rc2.at[0:3], bsem.at[10])
    wait(rm2.at[0:3], bsem.at[11])
    wait(rc3.at[0:3], bsem.at[12])
    wait(rm3.at[0:3], bsem.at[13])
    wait(zs.at[0:112], bsem.at[17])
    wait(zs.at[0:336], bsem.at[18])
    wait(tail.at[0, 0:48, :], bsem.at[19])
    wait(feat.at[0, 0:336, :], bsem.at[20])
    wait(feat.at[0:31], bsem.at[21])
    wait(feat.at[0, 0:192, :], bsem.at[22])
    wait(st.at[0:31], bsem.at[23])
    wait(tail.at[0:30], bsem.at[24])
    wait(zt.at[0:7], bsem.at[25])
    wait(fs.at[0:31], bsem.at[26])
    wait(fz.at[0:7], bsem.at[27])


def per_device(
    x_rows,
    attn_gain,
    final_gain,
    w_query,
    w_kv,
    w_out,
    kv_cache,
    w_vocab,
    token_ids,
    cache_len,
    row_traj,
):
    entries = w_vocab.shape[1]
    spread = np.exp(np.arange(HD // 2) * (-2.0 * math.log(rope_base) / HD)).astype(np.float32)
    vmem = pl.BlockSpec(memory_space=pltpu.VMEM)
    smem = pl.BlockSpec(memory_space=pltpu.SMEM)
    hbm = pl.BlockSpec(memory_space=pl.ANY)
    dma = pltpu.SemaphoreType.DMA
    attended, logprob = pl.pallas_call(
        kernel,
        out_shape=(
            jax.ShapeDtypeStruct((64, 256), BF16),
            jax.ShapeDtypeStruct((4, 128), F32),
        ),
        in_specs=[vmem, vmem, vmem, hbm, vmem, hbm, hbm, hbm, vmem, smem, vmem, vmem],
        out_specs=(vmem, vmem),
        scratch_shapes=[
            pltpu.VMEM((256, 1024), BF16),
            pltpu.VMEM((1024, 256), BF16),
            pltpu.VMEM((4, 1024, 256), BF16),
            pltpu.VMEM((4, 1024, 256), BF16),
            pltpu.VMEM((entries, 8192), BF16),
            pltpu.VMEM((16, 8192), BF16),
            pltpu.VMEM((512, 256), BF16),
            pltpu.VMEM((64, 256), BF16),
            pltpu.VMEM((512, 512), BF16),
            pltpu.VMEM((512, 512), BF16),
            pltpu.VMEM((512, 256), BF16),
            pltpu.VMEM((512, 1280), F32),
            pltpu.VMEM((256, 1280), F32),
            pltpu.VMEM((4, 64, 1280), BF16),
            pltpu.VMEM((4, 64, 1280), BF16),
            pltpu.VMEM((64, 1280), F32),
            pltpu.VMEM((4, 16, 1280), F32),
            pltpu.VMEM((512, 1280), BF16),
            pltpu.VMEM((512, 1024), F32),
            pltpu.VMEM((2, 512, 128), F32),
            pltpu.VMEM((256, 1024), F32),
            pltpu.VMEM((2, 256, 128), F32),
            pltpu.VMEM((4, 64, 1024), BF16),
            pltpu.VMEM((4, 2, 64, 128), F32),
            pltpu.VMEM((4, 64, 1024), BF16),
            pltpu.VMEM((4, 2, 64, 128), F32),
            pltpu.VMEM((64, 1024), F32),
            pltpu.VMEM((2, 64, 128), F32),
            pltpu.VMEM((4, 16, 1024), F32),
            pltpu.VMEM((4, 2, 16, 128), F32),
            pltpu.VMEM((512, 1024), BF16),
            pltpu.VMEM((512, 256), BF16),
            pltpu.VMEM((512, 256), BF16),
            pltpu.VMEM((8, 64, 256), BF16),
            pltpu.VMEM((32, 384, 256), BF16),
            pltpu.VMEM((32, 128, 256), BF16),
            pltpu.VMEM((512, entries), F32),
            pltpu.VMEM((512, 128), F32),
            pltpu.VMEM((32, 8, 128), F32),
            pltpu.VMEM((8, 8, 128), F32),
            pltpu.VMEM((32, 16, 128), F32),
            pltpu.VMEM((8, 16, 128), F32),
            dma((5,)),
            dma((28,)),
            dma((3,)),
            dma((4,)),
            dma((4,)),
            dma((4,)),
            dma((4,)),
            dma((4,)),
            dma((4,)),
            dma((2,)),
            dma((4,)),
            dma((8,)),
            dma((8,)),
            dma((4,)),
            dma((4,)),
            dma((2,)),
            dma((16,)),
            dma((8,)),
            dma((32,)),
            dma((32,)),
            dma((4,)),
            dma((4,)),
            dma((5,)),
            dma((5,)),
            dma((8,)),
            dma((8,)),
            dma((8,)),
        ],
        compiler_params=pltpu.CompilerParams(
            collective_id=0, has_side_effects=True, vmem_limit_bytes=60 * 1024 * 1024
        ),
        cost_estimate=pl.CostEstimate(
            flops=8_000_000_000, bytes_accessed=14_000_000, transcendentals=5_000_000
        ),
    )(
        x_rows,
        attn_gain.reshape(64, 128),
        final_gain.reshape(64, 128),
        w_query,
        w_kv,
        w_out,
        kv_cache,
        w_vocab.T,
        token_ids.reshape(4, 128),
        cache_len,
        row_traj.reshape(4, 128),
        jnp.asarray(np.concatenate([spread, spread])[None]),
    )
    return attended, logprob.reshape(-1)


def solution(mesh):
    in_specs = (
        P(("side", "seq"), None),
        P(),
        P(),
        P(("side", "seq"), "tensor"),
        P(("side", "seq"), None, "tensor"),
        P("tensor", ("side", "seq")),
        P(None, None, ("side", "seq"), "tensor"),
        P(None, ("side", "seq", "tensor")),
        P(),
        P(),
        P(),
    )
    out_specs = (P("tensor", ("side", "seq")), P())
    return jax.shard_map(
        per_device, mesh=mesh, in_specs=in_specs, out_specs=out_specs, check_vma=False
    )
```

```python
import functools
import math

import jax
import jax.numpy as jnp
import numpy as np
from jax import lax
from jax.experimental import pallas as pl
from jax.experimental.pallas import tpu as pltpu
from jax.sharding import PartitionSpec as P

HD = 128
TRAJ = 4
MESH = pl.DeviceIdType.MESH

epsilon = 1e-06
rope_base = 1000000.0
masked_low = -1e30
SCALE2 = float(HD) ** (-0.5) * math.log2(math.e)

F32 = jnp.float32
BF16 = jnp.bfloat16


def dot(a, b):
    return jnp.dot(a, b, preferred_element_type=F32)


def dot_nt(a, b):
    return lax.dot_general(a, b, (((1,), (1,)), ((), ())), preferred_element_type=F32)


def rows(start, size):
    return pl.ds(pl.multiple_of(start, size), size)


def column(row):
    return jnp.broadcast_to(row, (128, 128)).T


def merge(parts):
    top = functools.reduce(jnp.maximum, [p[1] for p in parts])
    factors = [jnp.exp2((p[1] - top) * SCALE2) for p in parts]
    mass = sum(p[2] * f for p, f in zip(parts, factors))
    outs = [
        sum(p[0](h) * f[:, h : h + 1] for p, f in zip(parts, factors)) for h in range(8)
    ]
    return outs, top, mass


def kernel(
    x_ref,
    ag_ref,
    fg_ref,
    wq_hbm,
    wkv_ref,
    wo_hbm,
    kv_hbm,
    wv_hbm,
    tok_ref,
    clen_ref,
    traj_ref,
    spread_ref,
    att_ref,
    lp_ref,
    wq,
    wo,
    keys,
    keys_t,
    values,
    wv,
    nx,
    xn,
    raw,
    place,
    place_t,
    xs,
    part,
    r1,
    s2,
    r2,
    sum2,
    r3,
    qkv,
    o_all,
    ml_all,
    rc1,
    rm1,
    sc2,
    sm2,
    rc2,
    rm2,
    oc2,
    mc2,
    rc3,
    rm3,
    ho,
    hpb,
    zs,
    zr,
    gz,
    feat,
    acc,
    st,
    zt,
    fs,
    lsem,
    bsem,
    asem,
    rawr,
    p1r,
    p2r,
    p3r,
    g1r,
    g2r,
    g3r,
    c1r,
    c2r,
    c3r,
    h1r,
    h2r,
    h3r,
    zrr,
    zgr,
    ftr,
    fbr,
    ztr,
    fsr,
):
    c = lax.axis_index("side")
    s = lax.axis_index("seq")
    z = lax.axis_index("tensor")
    j = c * 16 + s
    along = lax.div(s, 4)
    across = lax.rem(s, 4)
    a = along + c * (across - along)
    b = across + c * (along - across)
    row0 = c * 256 + a * 64 + b * 16

    def seq_of(side, a_, b_):
        straight = a_ * 4 + b_
        return straight + side * (b_ * 4 + a_ - straight)

    def blk(a_, b_):
        return c * 16 + seq_of(c, a_, b_)

    def peer(a_, b_):
        return (c, seq_of(c, a_, b_), z)

    def turn(v, k):
        return lax.rem(v + k, 4)

    sib = (1 - c, s, z)

    def send(src, dst, ssem, rsem, dev):
        pltpu.make_async_remote_copy(
            src_ref=src, dst_ref=dst, send_sem=ssem, recv_sem=rsem, device_id=dev, device_id_type=MESH
        ).start()

    def wait(ref, sem):
        pltpu.make_async_copy(ref, ref, sem).wait()

    def local(src, dst, n):
        return pltpu.make_async_copy(src, dst, lsem.at[n])

    copies = [
        local(wq_hbm, wq, 0),
        local(kv_hbm.at[0], keys, 1),
        local(kv_hbm.at[1], values.at[:, :, 0:128], 2),
        local(wo_hbm, wo, 3),
        local(wv_hbm, wv, 4),
    ]
    for copy in copies:
        copy.start()

    barrier = pltpu.get_barrier_semaphore()

    def greet(k, carry):
        i = lax.rem(j + k, 32)
        pl.semaphore_signal(barrier, inc=1, device_id=(lax.div(i, 16), lax.rem(i, 16), z), device_id_type=MESH)
        return carry

    lax.fori_loop(1, 32, greet, 0)

    def greet_z(k, carry):
        pl.semaphore_signal(barrier, inc=1, device_id=(c, s, lax.rem(z + k, 8)), device_id_type=MESH)
        return carry

    lax.fori_loop(1, 8, greet_z, 0)

    total = jnp.zeros((16, 1), F32)
    for n in range(8):
        v = x_ref[:, n * 1024 : (n + 1) * 1024].astype(F32)
        total = total + jnp.sum(v * v, axis=1, keepdims=True)
    unit = lax.rsqrt(total * (1.0 / 8192.0) + epsilon)
    for n in range(64):
        cols = slice(n * 128, (n + 1) * 128)
        v = x_ref[:, cols].astype(F32)
        nx[:, cols] = (v * unit * ag_ref[n : n + 1, :].astype(F32)).astype(BF16)

    pl.semaphore_wait(barrier, 38)

    def send_rows(k, carry):
        i = lax.rem(j + k, 32)
        send(
            nx.at[:, rows(i * 256, 256)],
            xn.at[rows(j * 16, 16), :],
            bsem.at[0],
            asem.at[0],
            (lax.div(i, 16), lax.rem(i, 16), z),
        )
        return carry

    lax.fori_loop(1, 32, send_rows, 0)
    xn[rows(j * 16, 16), :] = nx[:, rows(j * 256, 256)]

    traj = traj_ref[...].astype(F32)
    traj_cols = [column(traj[g : g + 1, :]) for g in range(4)]
    sub = lax.broadcasted_iota(jnp.int32, (128, 128), 0)
    lane = lax.broadcasted_iota(jnp.int32, (128, 128), 1)
    for g in range(4):
        step_col = jnp.zeros((128, 1), F32)
        step_row = jnp.zeros((1, 128), F32)
        for e in range(g + 1):
            same = jnp.where(traj_cols[g] == traj[e : e + 1, :], 1.0, 0.0)
            if e == g:
                same = jnp.where(lane < sub, same, 0.0)
            step_col = step_col + jnp.sum(same, axis=1, keepdims=True)
            same = jnp.where(traj_cols[e] == traj[g : g + 1, :], 1.0, 0.0)
            if e == g:
                same = jnp.where(sub < lane, same, 0.0)
            step_row = step_row + jnp.sum(same, axis=0, keepdims=True)
        slot_col = traj_cols[g] * 128.0 + step_col
        slot_row = traj[g : g + 1, :] * 128.0 + step_row
        for e in range(4):
            place_t[g * 128 : (g + 1) * 128, e * 128 : (e + 1) * 128] = jnp.where(
                (lane + e * 128).astype(F32) == slot_col, 1.0, 0.0
            ).astype(BF16)
            place[e * 128 : (e + 1) * 128, g * 128 : (g + 1) * 128] = jnp.where(
                (sub + e * 128).astype(F32) == slot_row, 1.0, 0.0
            ).astype(BF16)

    copies[1].wait()
    key_place = j * 1024 + lax.broadcasted_iota(jnp.int32, (128, 1024), 1)
    first_row = lax.broadcasted_iota(jnp.int32, (128, 1024), 0) == 0

    def turn_keys(t):
        keys_t[t, 0:128, :] = keys[t].T
        past = jnp.logical_and(first_row, key_place >= clen_ref[t])
        keys_t[t, 128:256, :] = jnp.where(past, masked_low, 0.0).astype(BF16)
        values[t, :, 128:256] = jnp.ones((1024, 128), BF16)

    turn_keys(0)
    turn_keys(1)

    own_traj = lax.div(row0, 128)
    own_step = lax.rem(row0, 128)
    cached = clen_ref[0]
    for t in range(1, 4):
        cached = jnp.where(own_traj == t, clen_ref[t], cached)
    lane16 = lane[0:16]
    angles = (cached + own_step + sub[0:16]).astype(F32) * spread_ref[...]
    cosine = jnp.cos(angles)
    sine = jnp.sin(angles)
    sine = jnp.where(lane16 < 64, -sine, sine)

    copies[0].wait()
    wait(xn.at[0:496], asem.at[0])

    def project(half):
        at = rows(half * 256, 256)
        xs[at, :] = dot(place[at, :], xn[...]).astype(BF16)
        part[at, 0:1024] = dot(xs[at, :], wq[...])
        part[at, 1024:1152] = dot(xs[at, :], wkv_ref[:, 0, :])
        part[at, 1152:1280] = dot(xs[at, :], wkv_ref[:, 1, :])

    project(1 - c)
    for k in (1, 2, 3, 0):
        q = turn(b, k)
        send(part.at[rows((1 - c) * 256 + q * 64, 64), :], r1.at[rows(q * 64, 64), :], bsem.at[2], p1r.at[q], sib)
    project(c)

    quarter = lax.rem(j, 4)
    holds_raw = lax.div(j, 4) == z

    @pl.when(holds_raw)
    def _():
        def send_raw(k, carry):
            i = lax.rem(j + k, 32)
            send(
                x_ref.at[:, rows(i * 256, 256)],
                raw.at[rows(quarter * 16, 16), :],
                bsem.at[1],
                rawr.at[quarter],
                (lax.div(i, 16), lax.rem(i, 16), z),
            )
            return carry

        lax.fori_loop(1, 32, send_raw, 0)
        raw[rows(quarter * 16, 16), :] = x_ref[:, rows(j * 256, 256)]

    turn_keys(2)

    def pair_sum(q):
        wait(r1.at[rows(q * 64, 64), :], p1r.at[q])
        return part[rows(c * 256 + q * 64, 64), :] + r1[rows(q * 64, 64), :]

    for k in (1, 2, 3):
        q = turn(a, k)
        s2[q] = pair_sum(q).astype(BF16)
        send(s2.at[q], r2.at[a], bsem.at[3], p2r.at[a], peer(q, b))
    sum2[...] = pair_sum(a)
    turn_keys(3)
    acc[...] = jnp.zeros(acc.shape, F32)
    for k in (3, 2, 1):
        q = turn(a, k)
        wait(r2.at[q], p2r.at[q])
        sum2[...] += r2[q].astype(F32)
    for k in (1, 2, 3):
        q = turn(b, k)
        send(sum2.at[rows(q * 16, 16), :], r3.at[b], bsem.at[4], p3r.at[b], peer(a, q))
    r3[b] = sum2[rows(b * 16, 16), :]
    for k in (3, 2, 1):
        q = turn(b, k)
        wait(r3.at[q], p3r.at[q])
    sums = (r3[0] + r3[1]) + (r3[2] + r3[3])
    mine = rows(row0, 16)
    for h in range(9):
        v = sums[:, h * 128 : (h + 1) * 128]
        qkv[mine, h * 128 : (h + 1) * 128] = (v * cosine + pltpu.roll(v, 64, 1) * sine).astype(BF16)
    qkv[mine, 1152:1280] = sums[:, 1152:1280].astype(BF16)

    a_up, a_down, a_far = turn(a, 1), turn(a, 3), turn(a, 2)
    b_up, b_down, b_far = turn(b, 1), turn(b, 3), turn(b, 2)

    def chunk(side, q):
        return rows(side * 256 + q * 64, 64)

    def half(q, n):
        return rows(c * 256 + q * 64 + n * 32, 32)

    def spread_start(ref, n, r_b, r_a, r_s):
        for k in (1, 2, 3):
            send(ref.at[mine, :], ref.at[mine, :], bsem.at[n], r_b.at[b], peer(a, turn(b, k)))
        for k in (3, 2, 1):
            q = turn(b, k)
            wait(ref.at[rows(c * 256 + a * 64 + q * 16, 16), :], r_b.at[q])
        at = ref.at[chunk(c, a), :]
        send(at, at, bsem.at[n + 1], r_a.at[a], peer(a_up, b))
        send(at, at, bsem.at[n + 1], r_a.at[a], peer(a_down, b))
        send(at, at, bsem.at[n + 2], r_s.at[a], sib)

    def spread_near(ref, n, r_a, r_s):
        for q, to, part_of, sem in ((a_down, a_up, 0, 0), (a_up, a_down, 1, 4)):
            at = ref.at[chunk(c, q), :]
            wait(at, r_a.at[q])
            at_half = ref.at[half(q, part_of), :]
            send(at_half, at_half, bsem.at[n + 1], r_a.at[q + sem], peer(to, b))
            send(at, at, bsem.at[n + 2], r_s.at[q], sib)

    def spread_far(ref, n, r_a, r_s):
        wait(ref.at[half(a_far, 0), :], r_a.at[a_far])
        wait(ref.at[half(a_far, 1), :], r_a.at[a_far + 4])
        at = ref.at[chunk(c, a_far), :]
        send(at, at, bsem.at[n + 2], r_s.at[a_far], sib)

    spread_start(qkv, 5, g1r, g2r, g3r)

    copies[2].wait()
    one = jnp.where(lax.broadcasted_iota(jnp.int32, (512, 128), 1) == 0, 1.0, 0.0).astype(BF16)
    lane64 = lane[0:64]

    def attend(side, q):
        at = chunk(side, q)
        t = side * 2 + lax.div(q, 2)
        heads = jnp.concatenate([qkv[at, h * 128 : (h + 1) * 128] for h in range(8)], axis=0)
        scores = dot(jnp.concatenate([heads, one], axis=1), keys_t[t])
        peak = jnp.max(scores, axis=1, keepdims=True)
        weights = jnp.exp2((scores - peak) * SCALE2).astype(BF16)
        out = dot(weights, values[t])
        peaks = jnp.zeros((64, 128), F32)
        masses = jnp.zeros((64, 128), F32)
        for h in range(8):
            head = slice(h * 64, (h + 1) * 64)
            o_all[at, h * 128 : (h + 1) * 128] = out[head, 0:128]
            peaks = jnp.where(lane64 == h, peak[head], peaks)
            masses = jnp.where(lane64 == h, out[head, 128:256], masses)
        ml_all[0, at, :] = peaks
        ml_all[1, at, :] = masses

    def attend_mine(n, carry):
        @pl.when(n == 1)
        def _():
            spread_near(qkv, 5, g2r, g3r)

        @pl.when(n == 2)
        def _():
            spread_far(qkv, 5, g2r, g3r)

        attend(c, turn(a, n))
        return carry

    def attend_other(n, carry):
        q = turn(b, jnp.where(n < 3, 2 - n, 3))
        wait(qkv.at[chunk(1 - c, q), :], g3r.at[q])
        attend(1 - c, q)
        at, to = chunk(1 - c, q), rows(q * 64, 64)
        send(o_all.at[at, :], rc1.at[to, :], bsem.at[8], c1r.at[q], sib)
        send(ml_all.at[:, at, :], rm1.at[:, to, :], bsem.at[9], c1r.at[q + 4], sib)
        return carry

    def join_pair(q):
        at, to = chunk(c, q), rows(q * 64, 64)
        wait(rc1.at[to, :], c1r.at[q])
        wait(rm1.at[:, to, :], c1r.at[q + 4])
        return merge(
            [
                (lambda h: o_all[at, h * 128 : (h + 1) * 128], ml_all[0, at, :], ml_all[1, at, :]),
                (lambda h: rc1[to, h * 128 : (h + 1) * 128], rm1[0, to, :], rm1[1, to, :]),
            ]
        )

    def send_joined(q):
        outs, top, mass = join_pair(q)
        for h in range(8):
            sc2[q, :, h * 128 : (h + 1) * 128] = outs[h].astype(BF16)
        sm2[q, 0] = top
        sm2[q, 1] = mass
        send(sc2.at[q], rc2.at[a], bsem.at[10], c2r.at[a], peer(q, b))
        send(sm2.at[q], rm2.at[a], bsem.at[11], c2r.at[a + 4], peer(q, b))

    lax.fori_loop(0, 3, attend_mine, 0)
    lax.fori_loop(0, 4, attend_other, 0)
    send_joined(a_far)
    send_joined(a_up)
    attend(c, a_down)
    send_joined(a_down)
    outs, top, mass = join_pair(a)
    for h in range(8):
        oc2[:, h * 128 : (h + 1) * 128] = outs[h]
    mc2[0] = top
    mc2[1] = mass

    own_rows = rows(own_traj * 128, 128)
    own_q = jnp.concatenate([qkv[mine, h * 128 : (h + 1) * 128] for h in range(8)], axis=0)
    own_scores = dot_nt(own_q, qkv[own_rows, 1024:1152])
    own_scores = jnp.where(lane <= own_step + (sub & 15), own_scores, masked_low)
    own_peak = jnp.max(own_scores, axis=1, keepdims=True)
    own_weights = jnp.exp2((own_scores - own_peak) * SCALE2)
    own_mass = jnp.sum(own_weights, axis=1, keepdims=True)
    own_out = dot(own_weights.astype(BF16), qkv[own_rows, 1152:1280])
    own_peaks = jnp.zeros((16, 128), F32)
    own_masses = jnp.zeros((16, 128), F32)
    for h in range(8):
        own_peaks = jnp.where(lane16 == h, own_peak[h * 16 : (h + 1) * 16], own_peaks)
        own_masses = jnp.where(lane16 == h, own_mass[h * 16 : (h + 1) * 16], own_masses)

    def arrived(k):
        q = turn(a, k)
        wait(rc2.at[q], c2r.at[q])
        wait(rm2.at[q], c2r.at[q + 4])
        return (lambda h: rc2[q, :, h * 128 : (h + 1) * 128].astype(F32), rm2[q, 0], rm2[q, 1])

    parts = [(lambda h: oc2[:, h * 128 : (h + 1) * 128], mc2[0], mc2[1])]
    parts += [arrived(k) for k in (2, 3, 1)]
    outs, top, mass = merge(parts)
    for h in range(8):
        oc2[:, h * 128 : (h + 1) * 128] = outs[h]
    mc2[0] = top
    mc2[1] = mass
    for k in (1, 2, 3):
        q = turn(b, k)
        send(oc2.at[rows(q * 16, 16), :], rc3.at[b], bsem.at[12], c3r.at[b], peer(a, q))
        send(mc2.at[:, rows(q * 16, 16), :], rm3.at[b], bsem.at[13], c3r.at[b + 4], peer(a, q))
    rc3[b] = oc2[rows(b * 16, 16), :]
    rm3[b] = mc2[:, rows(b * 16, 16), :]
    for k in (3, 2, 1):
        q = turn(b, k)
        wait(rc3.at[q], c3r.at[q])
        wait(rm3.at[q], c3r.at[q + 4])
    parts = [(lambda h, q=q: rc3[q, :, h * 128 : (h + 1) * 128], rm3[q, 0], rm3[q, 1]) for q in range(4)]
    parts.append((lambda h: own_out[h * 16 : (h + 1) * 16], own_peaks, own_masses))
    outs, top, mass = merge(parts)
    for h in range(8):
        ho[mine, h * 128 : (h + 1) * 128] = (outs[h] / mass[:, h : h + 1]).astype(BF16)

    spread_start(ho, 14, h1r, h2r, h3r)
    copies[3].wait()
    spread_near(ho, 14, h2r, h3r)
    spread_far(ho, 14, h2r, h3r)

    own_half = rows(c * 256, 256)
    hpb[own_half, :] = dot(ho[own_half, :], wo[...]).astype(BF16)
    for k in (0, 3, 1, 2):
        q = turn(b, k)
        wait(ho.at[chunk(1 - c, q), :], h3r.at[q])
    other_half = rows((1 - c) * 256, 256)
    hpb[other_half, :] = dot(ho[other_half, :], wo[...]).astype(BF16)

    def send_z(k, carry):
        q = lax.rem(z + k, 8)
        zs[q] = dot(place_t[rows(q * 64, 64), :], hpb[...]).astype(BF16)
        send(zs.at[q], zr.at[z], bsem.at[17], zrr.at[z], (c, s, q))
        return carry

    lax.fori_loop(1, 8, send_z, 0)
    total = dot(place_t[rows(z * 64, 64), :], hpb[...])
    for m in range(4):

        @pl.when(z * 4 + m != j)
        def _():
            wait(raw.at[rows(m * 16, 16), :], rawr.at[m])

    total = total + raw[...].astype(F32)
    for k in range(1, 8):
        q = lax.rem(z + 8 - k, 8)
        wait(zr.at[q], zrr.at[q])
        total = total + zr[q].astype(F32)
    attended = total.astype(BF16)
    att_ref[...] = attended
    attended = attended.astype(F32)
    my_z = rows(z * 64, 64)
    gains = fg_ref[...].astype(F32)
    gain_row = lax.broadcasted_iota(jnp.int32, (64, 128), 0)
    gain = [
        jnp.sum(jnp.where(gain_row == 2 * j + n, gains, 0.0), axis=0, keepdims=True) for n in (0, 1)
    ]
    gz[my_z, :] = (attended * jnp.concatenate(gain, axis=1)).astype(BF16)

    def send_feat_z(k, carry):
        ref = gz.at[my_z, :]
        send(ref, ref, bsem.at[18], zgr.at[z], (c, s, lax.rem(z + k, 8)))
        return carry

    lax.fori_loop(1, 8, send_feat_z, 0)

    squares = jnp.sum(attended * attended, axis=1, keepdims=True)
    squares = jnp.concatenate([jnp.broadcast_to(squares, (64, 128))] * 2, axis=0).T
    st[j] = squares[0:8]

    def send_squares(k, carry):
        i = lax.rem(j + k, 32)
        send(st.at[j], st.at[j], bsem.at[19], asem.at[1], (lax.div(i, 16), lax.rem(i, 16), z))
        return carry

    copies[4].wait()

    def multiply(*blocks):
        acc[...] += sum(dot(wv[:, rows(i * 256, 256)], feat[i]) for i in blocks)

    def send_block(i, dev):
        send(feat.at[i], feat.at[i], bsem.at[20], ftr.at[i], dev)

    def send_top(i, dev):
        send(feat.at[i, 0:128, :], feat.at[i, 0:128, :], bsem.at[20], ftr.at[i], dev)

    def send_bottom(i, dev):
        send(feat.at[i, 128:256, :], feat.at[i, 128:256, :], bsem.at[20], fbr.at[i], dev)

    def wait_halves(i):
        wait(feat.at[i, 0:128, :], ftr.at[i])
        wait(feat.at[i, 128:256, :], fbr.at[i])

    def fan(i):
        send_block(i, peer(a_up, b))
        send_block(i, peer(a_down, b))
        send_block(i, sib)

    def pass_chunk(k, carry):
        g = lax.rem(lax.div(z, 2) + jnp.where(k < 2, k, 5 - k), 4)
        for q in (2 * g, 2 * g + 1):

            @pl.when(q != z)
            def _():
                wait(gz.at[rows(q * 64, 64), :], zgr.at[q])

        at = rows(g * 128, 128)
        feat[j, :, at] = gz[at, :].T
        chunk = feat.at[j, :, at]
        for dev in (peer(a_up, b), peer(a_down, b), peer(a, b_up), peer(a, b_down), sib):
            send(chunk, chunk, bsem.at[20], ftr.at[j], dev)
        return carry

    lax.fori_loop(0, 4, pass_chunk, 0)
    i = blk(a, b_down)
    wait(feat.at[i], ftr.at[i])
    send_top(i, peer(a, b_up))
    fan(i)
    i = blk(a, b_up)
    wait(feat.at[i], ftr.at[i])
    send_bottom(i, peer(a, b_down))
    fan(i)

    for k in (8, 16, 24):
        send_squares(k, 0)
    i = blk(a, b_far)
    wait_halves(i)
    fan(i)

    def b_order(b_, n):
        step = jnp.where(n == 0, 0, jnp.where(n == 1, 3, n - 1))
        return lax.rem(b_ + step, 4)

    def sib_blk(a_, b_):
        return (1 - c) * 16 + seq_of(1 - c, a_, b_)

    def ready(i):
        wait(feat.at[i], ftr.at[i])
        return i

    def near(n, carry):
        bn = b_order(b, n)
        i = ready(blk(a_down, bn))
        send_top(i, peer(a_up, b))
        send_block(i, sib)
        k = ready(blk(a_up, bn))
        send_bottom(k, peer(a_down, b))
        send_block(k, sib)
        lax.fori_loop(8 * n + 1, 8 * n + 8, send_squares, 0)
        multiply(blk(a, bn), i, k, ready(sib_blk(b, b_order(a, n))))
        return carry

    lax.fori_loop(0, 4, near, 0)

    wait(st.at[0:31], asem.at[1])
    sum_sq = st[0]
    for n in range(1, 32):
        sum_sq = sum_sq + st[n]
    zt[z] = sum_sq

    def send_sum_sq(k, carry):
        send(zt.at[z], zt.at[z], bsem.at[21], ztr.at[z], (c, s, lax.rem(z + k, 8)))
        return carry

    lax.fori_loop(1, 8, send_sum_sq, 0)

    def far(n, carry):
        i = blk(a_far, b_order(b, n))
        wait_halves(i)
        send_block(i, sib)
        sn = b_order(a, n)
        multiply(i, ready(sib_blk(turn(b, 3), sn)), ready(sib_blk(turn(b, 1), sn)))
        return carry

    lax.fori_loop(0, 4, far, 0)

    def last(n, carry):
        multiply(*[ready(sib_blk(turn(b, 2), b_order(a, 2 * n + e))) for e in (0, 1)])
        return carry

    lax.fori_loop(0, 2, last, 0)

    for k in range(1, 8):
        q = lax.rem(z + 8 - k, 8)
        wait(zt.at[q], ztr.at[q])
    entries = acc.shape[0]
    offset = (j * 8 + z) * entries
    entry = offset + lax.broadcasted_iota(jnp.int32, (entries, 128), 0)
    for g in range(4):
        sum_sq = jnp.where(lane[0:1] < 64, zt[2 * g][0:1], zt[2 * g + 1][0:1])
        logits = acc[:, g * 128 : (g + 1) * 128] * lax.rsqrt(sum_sq * (1.0 / 8192.0) + epsilon)
        peak = jnp.max(logits, axis=0, keepdims=True)
        fs[c, g : g + 1, :] = peak
        fs[c, 4 + g : 5 + g, :] = jnp.sum(jnp.exp(logits - peak), axis=0, keepdims=True)
        fs[c, 8 + g : 9 + g, :] = jnp.sum(
            jnp.where(entry == tok_ref[g : g + 1, :], logits, 0.0), axis=0, keepdims=True
        )
    fs[c, 12:16, :] = jnp.zeros((4, 128), F32)

    def join_stats(stage, place_in, peers):
        count = len(peers) + 1
        base = stage * 8
        for dev in peers:
            ref = fs.at[base + place_in]
            send(ref, ref, bsem.at[22], fsr.at[base + place_in], dev)
        for k in range(1, count):
            at = base + lax.rem(place_in + k, count)
            wait(fs.at[at], fsr.at[at])
        top = fs[base, 0:4, :]
        for n in range(1, count):
            top = jnp.maximum(top, fs[base + n, 0:4, :])
        exp_total = jnp.zeros((4, 128), F32)
        picked_total = jnp.zeros((4, 128), F32)
        for n in range(count):
            exp_total = exp_total + fs[base + n, 4:8, :] * jnp.exp(fs[base + n, 0:4, :] - top)
            picked_total = picked_total + fs[base + n, 8:12, :]
        return top, exp_total, picked_total

    def keep_stats(at, stats):
        for n in range(3):
            fs[at, n * 4 : n * 4 + 4, :] = stats[n]
        fs[at, 12:16, :] = jnp.zeros((4, 128), F32)

    keep_stats(8 + along, join_stats(0, c, [sib]))
    keep_stats(16 + across, join_stats(1, along, [(c, turn(along, k) * 4 + across, z) for k in (1, 2, 3)]))
    keep_stats(24 + z, join_stats(2, across, [(c, along * 4 + turn(across, k), z) for k in (1, 2, 3)]))
    top, exp_total, picked_total = join_stats(3, z, [(c, s, lax.rem(z + k, 8)) for k in (4, 3, 5, 2, 6, 1, 7)])
    lp_ref[...] = picked_total - top - jnp.log(exp_total)

    wait(xn.at[0:496], bsem.at[0])

    @pl.when(holds_raw)
    def _():
        wait(xn.at[0:496], bsem.at[1])

    wait(r1, bsem.at[2])
    wait(r2.at[0:3], bsem.at[3])
    wait(r3.at[0:3], bsem.at[4])
    for ref, n in ((qkv, 5), (ho, 14)):
        wait(ref.at[0:48], bsem.at[n])
        wait(ref.at[0:192], bsem.at[n + 1])
        wait(ref.at[0:256], bsem.at[n + 2])
    wait(rc1, bsem.at[8])
    wait(rm1, bsem.at[9])
    wait(rc2.at[0:3], bsem.at[10])
    wait(rm2.at[0:3], bsem.at[11])
    wait(rc3.at[0:3], bsem.at[12])
    wait(rm3.at[0:3], bsem.at[13])
    wait(zr.at[0:7], bsem.at[17])
    wait(zr.at[0:7], bsem.at[18])
    wait(st.at[0:31], bsem.at[19])
    wait(feat.at[0:31], bsem.at[20])
    wait(zt.at[0:7], bsem.at[21])
    wait(fs.at[0:14], bsem.at[22])


def per_device(
    x_rows,
    attn_gain,
    final_gain,
    w_query,
    w_kv,
    w_out,
    kv_cache,
    w_vocab,
    token_ids,
    cache_len,
    row_traj,
):
    entries = w_vocab.shape[1]
    spread = np.exp(np.arange(HD // 2) * (-2.0 * math.log(rope_base) / HD)).astype(np.float32)
    vmem = pl.BlockSpec(memory_space=pltpu.VMEM)
    smem = pl.BlockSpec(memory_space=pltpu.SMEM)
    hbm = pl.BlockSpec(memory_space=pl.ANY)
    dma = pltpu.SemaphoreType.DMA
    attended, logprob = pl.pallas_call(
        kernel,
        out_shape=(
            jax.ShapeDtypeStruct((64, 256), BF16),
            jax.ShapeDtypeStruct((4, 128), F32),
        ),
        in_specs=[vmem, vmem, vmem, hbm, vmem, hbm, hbm, hbm, vmem, smem, vmem, vmem],
        out_specs=(vmem, vmem),
        scratch_shapes=[
            pltpu.VMEM((256, 1024), BF16),
            pltpu.VMEM((1024, 256), BF16),
            pltpu.VMEM((4, 1024, 128), BF16),
            pltpu.VMEM((4, 256, 1024), BF16),
            pltpu.VMEM((4, 1024, 256), BF16),
            pltpu.VMEM((entries, 8192), BF16),
            pltpu.VMEM((16, 8192), BF16),
            pltpu.VMEM((512, 256), BF16),
            pltpu.VMEM((64, 256), BF16),
            pltpu.VMEM((512, 512), BF16),
            pltpu.VMEM((512, 512), BF16),
            pltpu.VMEM((512, 256), BF16),
            pltpu.VMEM((512, 1280), F32),
            pltpu.VMEM((256, 1280), F32),
            pltpu.VMEM((4, 64, 1280), BF16),
            pltpu.VMEM((4, 64, 1280), BF16),
            pltpu.VMEM((64, 1280), F32),
            pltpu.VMEM((4, 16, 1280), F32),
            pltpu.VMEM((512, 1280), BF16),
            pltpu.VMEM((512, 1024), F32),
            pltpu.VMEM((2, 512, 128), F32),
            pltpu.VMEM((256, 1024), F32),
            pltpu.VMEM((2, 256, 128), F32),
            pltpu.VMEM((4, 64, 1024), BF16),
            pltpu.VMEM((4, 2, 64, 128), F32),
            pltpu.VMEM((4, 64, 1024), BF16),
            pltpu.VMEM((4, 2, 64, 128), F32),
            pltpu.VMEM((64, 1024), F32),
            pltpu.VMEM((2, 64, 128), F32),
            pltpu.VMEM((4, 16, 1024), F32),
            pltpu.VMEM((4, 2, 16, 128), F32),
            pltpu.VMEM((512, 1024), BF16),
            pltpu.VMEM((512, 256), BF16),
            pltpu.VMEM((8, 64, 256), BF16),
            pltpu.VMEM((8, 64, 256), BF16),
            pltpu.VMEM((512, 256), BF16),
            pltpu.VMEM((32, 256, 512), BF16),
            pltpu.VMEM((entries, 512), F32),
            pltpu.VMEM((32, 8, 128), F32),
            pltpu.VMEM((8, 8, 128), F32),
            pltpu.VMEM((32, 16, 128), F32),
            dma((5,)),
            dma((23,)),
            dma((2,)),
            dma((4,)),
            dma((4,)),
            dma((4,)),
            dma((4,)),
            dma((4,)),
            dma((8,)),
            dma((4,)),
            dma((8,)),
            dma((8,)),
            dma((8,)),
            dma((4,)),
            dma((8,)),
            dma((4,)),
            dma((8,)),
            dma((8,)),
            dma((32,)),
            dma((32,)),
            dma((8,)),
            dma((32,)),
        ],
        compiler_params=pltpu.CompilerParams(
            collective_id=0, has_side_effects=True, vmem_limit_bytes=60 * 1024 * 1024
        ),
        cost_estimate=pl.CostEstimate(
            flops=8_000_000_000, bytes_accessed=14_000_000, transcendentals=5_000_000
        ),
    )(
        x_rows,
        attn_gain.reshape(64, 128),
        final_gain.reshape(64, 128),
        w_query,
        w_kv,
        w_out,
        kv_cache,
        w_vocab.T,
        token_ids.reshape(4, 128),
        cache_len,
        row_traj.reshape(4, 128),
        jnp.asarray(np.concatenate([spread, spread])[None]),
    )
    return attended, logprob.reshape(-1)


def solution(mesh):
    in_specs = (
        P(("side", "seq"), None),
        P(),
        P(),
        P(("side", "seq"), "tensor"),
        P(("side", "seq"), None, "tensor"),
        P("tensor", ("side", "seq")),
        P(None, None, ("side", "seq"), "tensor"),
        P(None, ("side", "seq", "tensor")),
        P(),
        P(),
        P(),
    )
    out_specs = (P("tensor", ("side", "seq")), P())
    return jax.shard_map(
        per_device, mesh=mesh, in_specs=in_specs, out_specs=out_specs, check_vma=False
    )
```

```python
import functools
import math

import jax
import jax.numpy as jnp
import numpy as np
from jax import lax
from jax.experimental import pallas as pl
from jax.experimental.pallas import tpu as pltpu
from jax.sharding import PartitionSpec as P

HD = 128
TRAJ = 4
MESH = pl.DeviceIdType.MESH

epsilon = 1e-06
rope_base = 1000000.0
masked_low = -1e30
SCALE2 = float(HD) ** (-0.5) * math.log2(math.e)

F32 = jnp.float32
BF16 = jnp.bfloat16


def dot(a, b):
    return jnp.dot(a, b, preferred_element_type=F32)


def dot_nt(a, b):
    return lax.dot_general(a, b, (((1,), (1,)), ((), ())), preferred_element_type=F32)


def rows(start, size):
    return pl.ds(pl.multiple_of(start, size), size)


def column(row):
    return jnp.broadcast_to(row, (128, 128)).T


def merge(parts):
    top = functools.reduce(jnp.maximum, [p[1] for p in parts])
    factors = [jnp.exp2((p[1] - top) * SCALE2) for p in parts]
    mass = sum(pltpu.roll(p[1], 120, 1) * f for p, f in zip(parts, factors))
    outs = [
        sum(p[0](h) * f[:, h : h + 1] for p, f in zip(parts, factors)) for h in range(8)
    ]
    return outs, top, mass


def pack(top, mass):
    lane = lax.broadcasted_iota(jnp.int32, top.shape, 1)
    return jnp.where(lane < 8, top, jnp.where(lane < 16, pltpu.roll(mass, 8, 1), 0.0))


def encode(stats):
    lane = lax.broadcasted_iota(jnp.int32, stats.shape, 1)
    high = stats.astype(BF16).astype(F32)
    middle = (stats - high).astype(BF16).astype(F32)
    low = (stats - high) - middle
    terms = jnp.where(lane < 32, pltpu.roll(middle, 16, 1), pltpu.roll(low, 32, 1))
    return jnp.where(lane < 16, high, jnp.where(lane < 48, terms, 0.0)).astype(BF16)


def decode(terms):
    terms = terms.astype(F32)
    return (terms + pltpu.roll(terms, 112, 1)) + pltpu.roll(terms, 96, 1)


def kernel(
    x_ref,
    ag_ref,
    fg_ref,
    wq_hbm,
    wkv_ref,
    wo_hbm,
    kv_hbm,
    wv_hbm,
    tok_ref,
    clen_ref,
    traj_ref,
    spread_ref,
    att_ref,
    lp_ref,
    wq,
    wo,
    keys,
    keys_t,
    values,
    wv,
    wv_sib,
    nx,
    xn,
    raw,
    raw_s,
    place,
    place_t,
    toks,
    trig,
    xs,
    part,
    r1,
    s2,
    r2,
    x3,
    r3,
    qkv,
    o_all,
    rc1,
    sc2,
    rc2,
    oc2,
    mc2,
    rc3,
    ho,
    hp,
    hpb,
    zr,
    attz,
    feat,
    acc,
    racc,
    st,
    fs,
    fz,
    lsem,
    bsem,
    asem,
    p1r,
    p2r,
    p3r,
    g2r,
    g3r,
    c1r,
    c2r,
    c3r,
    h2r,
    h3r,
    zrr,
    zgr,
    ftr,
    fbr,
    wvr,
    rar,
):
    c = lax.axis_index("side")
    s = lax.axis_index("seq")
    z = lax.axis_index("tensor")
    j = c * 16 + s
    along = lax.div(s, 4)
    across = lax.rem(s, 4)
    a = along + c * (across - along)
    b = across + c * (along - across)

    def seq_of(side, a_, b_):
        straight = a_ * 4 + b_
        return straight + side * (b_ * 4 + a_ - straight)

    def blk(a_, b_):
        return seq_of(c, a_, b_)

    def peer(a_, b_):
        return (c, seq_of(c, a_, b_), z)

    def turn(v, k):
        return lax.rem(v + k, 4)

    sib = (1 - c, s, z)

    def plane(k):
        i = lax.rem(j + k, 32)
        return i, (lax.div(i, 16), lax.rem(i, 16), z)

    def column_of(k):
        q = lax.rem(z + k, 8)
        return q, (c, s, q)

    def send(src, dst, ssem, rsem, dev):
        pltpu.make_async_remote_copy(
            src_ref=src, dst_ref=dst, send_sem=ssem, recv_sem=rsem, device_id=dev, device_id_type=MESH
        ).start()

    def wait(ref, sem):
        pltpu.make_async_copy(ref, ref, sem).wait()

    def local(src, dst, n):
        return pltpu.make_async_copy(src, dst, lsem.at[n])

    def each(low, high, body):
        def step(k, carry):
            body(k)
            return carry

        lax.fori_loop(low, high, step, 0)

    copies = [
        local(wq_hbm, wq, 0),
        local(kv_hbm.at[0], keys, 1),
        local(kv_hbm.at[1], values.at[:, :, 0:128], 2),
        local(wo_hbm, wo, 3),
        local(wv_hbm.at[:, rows(c * 4096, 4096)], wv, 4),
    ]
    for copy in copies:
        copy.start()

    barrier = pltpu.get_barrier_semaphore()

    def greet(k):
        pl.semaphore_signal(barrier, inc=1, device_id=plane(k)[1], device_id_type=MESH)

    def greet_z(k):
        pl.semaphore_signal(barrier, inc=1, device_id=column_of(k)[1], device_id_type=MESH)

    each(1, 32, greet)
    each(1, 8, greet_z)

    def greet_sib_z(k):
        q, _ = column_of(k)
        pl.semaphore_signal(barrier, inc=1, device_id=(1 - c, s, q), device_id_type=MESH)

    each(1, 8, greet_sib_z)

    total = jnp.zeros((16, 1), F32)
    for n in range(8):
        v = x_ref[:, n * 1024 : (n + 1) * 1024].astype(F32)
        total = total + jnp.sum(v * v, axis=1, keepdims=True)
    unit = lax.rsqrt(total * (1.0 / 8192.0) + epsilon)
    for n in range(64):
        cols = slice(n * 128, (n + 1) * 128)
        v = x_ref[:, cols].astype(F32)
        nx[:, cols] = (v * unit * ag_ref[n : n + 1, :].astype(F32)).astype(BF16)

    pl.semaphore_wait(barrier, 45)

    def send_weights(n):
        send(
            wv_hbm.at[:, rows((1 - c) * 4096 + n * 1024, 1024)],
            wv_sib.at[:, n * 1024 : (n + 1) * 1024],
            bsem.at[28],
            wvr.at[n],
            sib,
        )

    here = rows(j * 16, 16)

    def send_rows(k):
        i, dev = plane(k)
        send(nx.at[:, rows(i * 256, 256)], xn.at[here, :], bsem.at[0], asem.at[0], dev)

    def send_raw(k):
        i, dev = plane(k)
        send(x_ref.at[:, rows(i * 256, 256)], raw.at[here, :], bsem.at[1], asem.at[1], dev)

    each(1, 32, send_rows)
    xn[here, :] = nx[:, rows(j * 256, 256)]
    raw[here, :] = x_ref[:, rows(j * 256, 256)]

    traj = traj_ref[...].astype(F32)
    traj_cols = [column(traj[g : g + 1, :]) for g in range(4)]
    sub = lax.broadcasted_iota(jnp.int32, (128, 128), 0)
    lane = lax.broadcasted_iota(jnp.int32, (128, 128), 1)
    for g in range(4):
        step_col = jnp.zeros((128, 1), F32)
        step_row = jnp.zeros((1, 128), F32)
        for e in range(g + 1):
            same = jnp.where(traj_cols[g] == traj[e : e + 1, :], 1.0, 0.0)
            if e == g:
                same = jnp.where(lane < sub, same, 0.0)
            step_col = step_col + jnp.sum(same, axis=1, keepdims=True)
            same = jnp.where(traj_cols[e] == traj[g : g + 1, :], 1.0, 0.0)
            if e == g:
                same = jnp.where(sub < lane, same, 0.0)
            step_row = step_row + jnp.sum(same, axis=0, keepdims=True)
        slot_col = traj_cols[g] * 128.0 + step_col
        slot_row = traj[g : g + 1, :] * 128.0 + step_row
        for e in range(4):
            place_t[g * 128 : (g + 1) * 128, e * 128 : (e + 1) * 128] = jnp.where(
                (lane + e * 128).astype(F32) == slot_col, 1.0, 0.0
            ).astype(BF16)
            place[e * 128 : (e + 1) * 128, g * 128 : (g + 1) * 128] = jnp.where(
                (sub + e * 128).astype(F32) == slot_row, 1.0, 0.0
            ).astype(BF16)

    key_place = j * 1024 + lax.broadcasted_iota(jnp.int32, (128, 1024), 1)
    first_row = lax.broadcasted_iota(jnp.int32, (128, 1024), 0) == 0

    def turn_keys(t):
        keys_t[t, 0:128, :] = keys[t].T
        past = jnp.logical_and(first_row, key_place >= clen_ref[t])
        keys_t[t, 128:256, :] = jnp.where(past, masked_low, 0.0).astype(BF16)
        values[t, :, 128:256] = jnp.ones((1024, 128), BF16)

    copies[0].wait()
    wait(xn.at[0:496], asem.at[0])

    def project(half):
        at = rows(half * 256, 256)
        xs[at, :] = dot(place[at, :], xn[...]).astype(BF16)
        part[at, 0:1024] = dot(xs[at, :], wq[...])
        part[at, 1024:1152] = dot(xs[at, :], wkv_ref[:, 0, :])
        part[at, 1152:1280] = dot(xs[at, :], wkv_ref[:, 1, :])

    def group(side, p):
        return rows((side * 2 + p // 2) * 128 + (p % 2) * 64, 64)

    def slab(p, q):
        return rows((c * 2 + p // 2) * 128 + (p % 2) * 64 + q * 16, 16)

    project(1 - c)
    for p in range(4):
        send(part.at[group(1 - c, p), :], r1.at[p], bsem.at[4 + p], p1r.at[p], sib)
    each(1, 16, send_raw)
    project(c)
    each(16, 32, send_raw)

    def reduce_a(p):
        wait(r1.at[p], p1r.at[p])
        for k in (2, 1, 3):
            q = turn(a, k)
            s2[p, q] = (part[slab(p, q), :] + r1[p, rows(q * 16, 16), :]).astype(BF16)
            send(s2.at[p, q], r2.at[p, a], bsem.at[8 + p], p2r.at[p * 4 + a], peer(q, b))
        x3[p] = part[slab(p, a), :] + r1[p, rows(a * 16, 16), :]

    def reduce_b(p):
        for k in (1, 3, 2):
            q = turn(a, k)
            wait(r2.at[p, q], p2r.at[p * 4 + q])
            x3[p] += r2[p, q].astype(F32)
        for k in (2, 1, 3):
            send(x3.at[p], r3.at[p, b], bsem.at[12 + p], p3r.at[p * 4 + b], peer(a, turn(b, k)))
        r3[p, b] = x3[p]

    def rotate(p):
        for k in (1, 3, 2):
            q = turn(b, k)
            wait(r3.at[p, q], p3r.at[p * 4 + q])
        at = slab(p, a)
        cosine, sine = trig[p, 0], trig[p, 1]
        for h in range(10):
            cols = slice(h * 128, (h + 1) * 128)
            v = (r3[p, 0, :, cols] + r3[p, 1, :, cols]) + (r3[p, 2, :, cols] + r3[p, 3, :, cols])
            if h < 9:
                v = v * cosine + pltpu.roll(v, 64, 1) * sine
            qkv[at, cols] = v.astype(BF16)

    def gather_a(p, ref, n, sems):
        ref = ref.at[slab(p, a), :]
        for k in (2, 1, 3):
            send(ref, ref, bsem.at[2 * n + p], sems.at[p * 4 + a], peer(turn(a, k), b))

    def gather_sib(p, ref, n, sems, to):
        for k in (1, 3, 2):
            q = turn(a, k)
            wait(ref.at[slab(p, q), :], sems.at[p * 4 + q])
        ref = ref.at[group(c, p), :]
        send(ref, ref, bsem.at[2 * n + p], to.at[p], sib)

    lane16 = lane[0:16]

    def angles():
        for p in range(4):
            cached = jnp.where(c == 0, clen_ref[p // 2], clen_ref[2 + p // 2])
            turned = (cached + (p % 2) * 64 + a * 16 + sub[0:16]).astype(F32) * spread_ref[...]
            trig[p, 0] = jnp.cos(turned)
            sine = jnp.sin(turned)
            trig[p, 1] = jnp.where(lane16 < 64, -sine, sine)

    def z_rows(p, q):
        return rows((lax.div(q, 4) * 2 + p // 2) * 128 + (p % 2) * 64 + lax.rem(q, 4) * 16, 16)


    def group_raw():
        wait(raw.at[0:496], asem.at[1])
        for p in range(4):
            raw_s[p] = dot(place[z_rows(p, z), :], raw[...])

    def group_tokens():
        token = tok_ref[...].astype(F32)
        token_cols = [column(token[g : g + 1, :]) for g in range(4)]
        grouped = [
            sum(
                jnp.sum(
                    place_t[g * 128 : (g + 1) * 128, t * 128 : (t + 1) * 128].astype(F32) * token_cols[g],
                    axis=0,
                    keepdims=True,
                )
                for g in range(4)
            )
            for t in range(4)
        ]
        for p in range(4):
            first, second = grouped[p // 2], grouped[2 + p // 2]
            if p % 2 == 0:
                toks[p : p + 1, :] = jnp.where(lane[0:1] < 64, first, pltpu.roll(second, 64, 1))
            else:
                toks[p : p + 1, :] = jnp.where(lane[0:1] < 64, pltpu.roll(first, 64, 1), second)
        acc[...] = jnp.zeros(acc.shape, F32)

    one = jnp.where(lax.broadcasted_iota(jnp.int32, (256, 128), 1) == 0, 1.0, 0.0).astype(BF16)
    lane64 = lane[0:64]

    def attend(side, p):
        at = group(side, p)
        t = side * 2 + p // 2
        stats = jnp.zeros((64, 128), F32)
        for h in range(0, 8, 4):
            heads = jnp.concatenate(
                [qkv[at, (h + e) * 128 : (h + e + 1) * 128] for e in range(4)], axis=0
            )
            scores = dot(jnp.concatenate([heads, one], axis=1), keys_t[t])
            peak = jnp.max(scores, axis=1, keepdims=True)
            weights = jnp.exp2((scores - peak) * SCALE2).astype(BF16)
            out = dot(weights, values[t])
            for e in range(4):
                head = slice(e * 64, (e + 1) * 64)
                o_all[at, (h + e) * 128 : (h + e + 1) * 128] = out[head, 0:128]
                stats = jnp.where(lane64 == h + e, peak[head], stats)
                stats = jnp.where(lane64 == 8 + h + e, out[head, 128:256], stats)
        o_all[at, 1024:1152] = stats

    def attend_sib(p):
        at = group(1 - c, p)
        wait(qkv.at[at, :], g3r.at[p])
        attend(1 - c, p)
        send(o_all.at[at, :], rc1.at[p], bsem.at[24 + p], c1r.at[p], sib)

    def join_a(p):
        wait(rc1.at[p], c1r.at[p])

        def joined(q):
            at, to = slab(p, q), rows(q * 16, 16)
            return merge(
                [
                    (lambda h: o_all[at, h * 128 : (h + 1) * 128], o_all[at, 1024:1152]),
                    (lambda h: rc1[p, to, h * 128 : (h + 1) * 128], rc1[p, to, 1024:1152]),
                ]
            )

        for k in (2, 1, 3):
            q = turn(a, k)
            outs, top, mass = joined(q)
            for h in range(8):
                sc2[p, q, :, h * 128 : (h + 1) * 128] = outs[h].astype(BF16)
            sc2[p, q, :, 1024:1152] = encode(pack(top, mass))
            send(sc2.at[p, q], rc2.at[p, a], bsem.at[32 + p], c2r.at[p * 4 + a], peer(q, b))
        outs, top, mass = joined(a)
        for h in range(8):
            oc2[p, :, h * 128 : (h + 1) * 128] = outs[h]
        mc2[p] = pack(top, mass)

    def join_b(p):
        def arrived(k):
            q = turn(a, k)
            wait(rc2.at[p, q], c2r.at[p * 4 + q])
            return (lambda h: rc2[p, q, :, h * 128 : (h + 1) * 128].astype(F32), decode(rc2[p, q, :, 1024:1152]))

        parts = [(lambda h: oc2[p, :, h * 128 : (h + 1) * 128], mc2[p])]
        parts += [arrived(k) for k in (1, 3, 2)]
        outs, top, mass = merge(parts)
        for h in range(8):
            rc3[p, b, :, h * 128 : (h + 1) * 128] = outs[h].astype(BF16)
        rc3[p, b, :, 1024:1152] = encode(pack(top, mass))
        for k in (2, 1, 3):
            dev = peer(a, turn(b, k))
            send(rc3.at[p, b], rc3.at[p, b], bsem.at[40 + p], c3r.at[p * 4 + b], dev)

    def join_own(p):
        at = slab(p, a)
        count = 64 * (1 + p % 2)
        keys_at = rows((c * 2 + p // 2) * 128, count)
        own_q = jnp.concatenate([qkv[at, h * 128 : (h + 1) * 128] for h in range(8)], axis=0)
        scores = dot_nt(own_q, qkv[keys_at, 1024:1152])
        step = lax.broadcasted_iota(jnp.int32, (128, count), 0) & 15
        key = lax.broadcasted_iota(jnp.int32, (128, count), 1)
        scores = jnp.where(key <= (p % 2) * 64 + a * 16 + step, scores, masked_low)
        peak = jnp.max(scores, axis=1, keepdims=True)
        weights = jnp.exp2((scores - peak) * SCALE2)
        mass = jnp.sum(weights, axis=1, keepdims=True)
        out = dot(weights.astype(BF16), qkv[keys_at, 1152:1280])
        stats = jnp.zeros((16, 128), F32)
        for h in range(8):
            head = slice(h * 16, (h + 1) * 16)
            stats = jnp.where(lane16 == h, peak[head], stats)
            stats = jnp.where(lane16 == 8 + h, mass[head], stats)
        for k in (1, 3, 2):
            q = turn(b, k)
            wait(rc3.at[p, q], c3r.at[p * 4 + q])
        parts = [
            (lambda h, q=q: rc3[p, q, :, h * 128 : (h + 1) * 128].astype(F32), decode(rc3[p, q, :, 1024:1152]))
            for q in range(4)
        ]
        parts.append((lambda h: out[h * 16 : (h + 1) * 16], stats))
        outs, top, mass = merge(parts)
        for h in range(8):
            ho[at, h * 128 : (h + 1) * 128] = (outs[h] / mass[:, h : h + 1]).astype(BF16)
        gather_a(p, ho, 24, h2r)

    def project_out(p):
        def half(side):
            at = group(side, p)
            hp[at, :] = dot(ho[at, :], wo[...])
            hpb[at, :] = hp[at, :].astype(BF16)

        half(c)
        wait(ho.at[group(1 - c, p), :], h3r.at[p])
        half(1 - c)

        def send_z(k):
            q, dev = column_of(lax.rem(4 + lax.div(k, 2) * (1 - 2 * lax.rem(k, 2)) + 8, 8))
            send(hpb.at[z_rows(p, q), :], zr.at[p, z], bsem.at[56 + p], zrr.at[p * 8 + z], dev)

        each(1, 8, send_z)

    def attended(p):
        my_z = z_rows(p, z)
        total = raw_s[p] + hp[my_z, :]
        for k in (1, 7, 2, 6, 3, 5, 4):
            q = lax.rem(z + k, 8)
            wait(zr.at[p, q], zrr.at[p * 8 + q])
            total = total + zr[p, q].astype(F32)
        attz[my_z, :] = total.astype(BF16)

        def send_z(k):
            q, dev = column_of(lax.rem(4 + lax.div(k, 2) * (1 - 2 * lax.rem(k, 2)) + 8, 8))
            ref = attz.at[my_z, :]
            send(ref, ref, bsem.at[60 + p], zgr.at[p * 8 + z], dev)

        each(1, 8, send_z)

    a_up, a_down, a_far = turn(a, 1), turn(a, 3), turn(a, 2)
    b_up, b_down, b_far = turn(b, 1), turn(b, 3), turn(b, 2)

    gains = fg_ref[...].astype(F32)
    gain_row = lax.broadcasted_iota(jnp.int32, (64, 128), 0)
    gain_col = jnp.concatenate(
        [
            column(jnp.sum(jnp.where(gain_row == 2 * j + n, gains, 0.0), axis=0, keepdims=True))
            for n in (0, 1)
        ],
        axis=0,
    )

    def features(p):
        for k in (1, 7, 2, 6, 3, 5, 4):
            q = lax.rem(z + k, 8)
            wait(attz.at[z_rows(p, q), :], zgr.at[p * 8 + q])
        turned = jnp.concatenate([attz[group(0, p), :], attz[group(1, p), :]], axis=0).T.astype(F32)
        st[j, p : p + 1, :] = jnp.sum(turned * turned, axis=0, keepdims=True)
        feat[p // 2, s, :, lanes(p)] = (turned * gain_col).astype(BF16)
        for dev in (peer(a_up, b), peer(a_down, b), peer(a, b_up), peer(a, b_down)):
            send_block(p, s, dev)

    def send_squares(k):
        send(st.at[j], st.at[j], bsem.at[68], asem.at[2], plane(k)[1])

    def multiply(pair, *blocks):
        acc[0, pair] += sum(dot(wv[:, rows(i * 256, 256)], feat[pair, i]) for i in blocks)
        acc[1, pair] += sum(dot(wv_sib[:, rows(i * 256, 256)], feat[pair, i]) for i in blocks)

    def lanes(p):
        return slice((p % 2) * 128, (p % 2) * 128 + 128)

    def block(p, i):
        return feat.at[p // 2, i, :, lanes(p)]

    def top(p, i):
        return feat.at[p // 2, i, 0:128, lanes(p)]

    def bottom(p, i):
        return feat.at[p // 2, i, 128:256, lanes(p)]

    def send_block(p, i, dev):
        send(block(p, i), block(p, i), bsem.at[64 + p], ftr.at[p * 16 + i], dev)

    def send_top(p, i, dev):
        send(top(p, i), top(p, i), bsem.at[64 + p], ftr.at[p * 16 + i], dev)

    def send_bottom(p, i, dev):
        send(bottom(p, i), bottom(p, i), bsem.at[64 + p], fbr.at[p * 16 + i], dev)

    def ready(p, i):
        wait(block(p, i), ftr.at[p * 16 + i])
        return i

    def wait_halves(p, i):
        wait(top(p, i), ftr.at[p * 16 + i])
        wait(bottom(p, i), fbr.at[p * 16 + i])

    def fan(p, i):
        send_block(p, i, peer(a_up, b))
        send_block(p, i, peer(a_down, b))

    def pass_b(p):
        i = ready(p, blk(a, b_down))
        send_top(p, i, peer(a, b_up))
        fan(p, i)
        i = ready(p, blk(a, b_up))
        send_bottom(p, i, peer(a, b_down))
        fan(p, i)
        i = blk(a, b_far)
        wait_halves(p, i)
        fan(p, i)

    def order(b_, n):
        step = jnp.where(n == 0, 0, jnp.where(n == 1, 3, n - 1))
        return lax.rem(b_ + step, 4)

    def near(p):
        def step(n):
            bn = order(b, n)
            i = ready(p, blk(a_down, bn))
            send_top(p, i, peer(a_up, b))
            k = ready(p, blk(a_up, bn))
            send_bottom(p, k, peer(a_down, b))
            if p == 2:
                each(8 * n + 1, 8 * n + 8, send_squares)
            if p % 2 == 1:
                multiply(p // 2, blk(a, bn), i, k)

        each(0, 4, step)

    def far(p):
        def step(n):
            blocks = [blk(a_far, order(b, 2 * n + e)) for e in (0, 1)]
            for i in blocks:
                wait_halves(p, i)
            if p % 2 == 1:
                multiply(p // 2, *blocks)

        each(0, 2, step)
        if p % 2 == 1:
            send(acc.at[1, p // 2], racc.at[p // 2], bsem.at[36 + p // 2], rar.at[p // 2], sib)

    entries = acc.shape[2]
    offset = (j * 8 + z) * entries
    slot = c * 8 + z

    def statistics(pair, sum_sq):
        wait(racc.at[pair], rar.at[pair])
        entry = (offset + lax.broadcasted_iota(jnp.int32, (entries, 128), 0)).astype(F32)
        for g in (0, 1):
            n = pair * 2 + g
            cols = slice(g * 128, (g + 1) * 128)
            logits = (acc[0, pair, :, cols] + racc[pair, :, cols]) * lax.rsqrt(
                sum_sq[n : n + 1] * (1.0 / 8192.0) + epsilon
            )
            peak = jnp.max(logits, axis=0, keepdims=True)
            fs[slot, n : n + 1, :] = peak
            fs[slot, 4 + n : 5 + n, :] = jnp.sum(jnp.exp(logits - peak), axis=0, keepdims=True)
            fs[slot, 8 + n : 9 + n, :] = jnp.sum(
                jnp.where(entry == toks[n : n + 1, :], logits, 0.0), axis=0, keepdims=True
            )

    def start_attention(p):
        gather_sib(p, qkv, 10, g2r, g3r)
        attend(c, p)

    def start_gather(p):
        rotate(p)
        gather_a(p, qkv, 8, g2r)

    def share_heads(p):
        gather_sib(p, ho, 26, h2r, h3r)

    stages = (
        reduce_a,
        reduce_b,
        start_gather,
        start_attention,
        attend_sib,
        join_a,
        join_b,
        join_own,
        share_heads,
        project_out,
        attended,
        features,
        pass_b,
        near,
        far,
    )
    for time in range(len(stages) + 3):
        work = [(time - p, p) for p in range(4) if 0 <= time - p < len(stages)]
        work = [w for w in work if w[0] < 12] + [w for w in work[::-1] if w[0] >= 12]
        for stage, p in work:
            if stage == 13 and p == 0:
                copies[4].wait()
                for n in range(4):
                    wait(wv_sib.at[:, n * 1024 : (n + 1) * 1024], wvr.at[n])
            if stage == 14 and p == 3:
                wait(st.at[0:31], asem.at[2])
                sum_sq = st[0]
                for n in range(1, 32):
                    sum_sq = sum_sq + st[n]
                statistics(0, sum_sq)
            stages[stage](p)
        if time == 0:
            send_weights(0)
            angles()
            copies[1].wait()
            turn_keys(c * 2)
        elif time == 1:
            send_weights(1)
            turn_keys((1 - c) * 2)
            copies[2].wait()
        elif time == 2:
            turn_keys(c * 2 + 1)
        elif time == 3:
            turn_keys((1 - c) * 2 + 1)
        elif time == 5:
            send_weights(2)
        elif time == 6:
            send_weights(3)
            copies[3].wait()
        elif time == 7:
            group_raw()
        elif time == 8:
            group_tokens()
        elif time == 14:
            for k in (8, 16, 24):
                send_squares(k)
            att_ref[...] = dot(place_t[rows(z * 64, 64), :], attz[...]).astype(BF16)
    statistics(1, sum_sq)
    fs[slot, 12:16, :] = jnp.zeros((4, 128), F32)

    def send_stats(k):
        i = lax.rem(slot + k, 16)
        send(fs.at[slot], fs.at[slot], bsem.at[70], asem.at[3], (lax.div(i, 8), s, lax.rem(i, 8)))

    each(1, 16, send_stats)

    def join_stats(ref, count):
        top = ref[0, 0:4, :]
        for n in range(1, count):
            top = jnp.maximum(top, ref[n, 0:4, :])
        exp_total = jnp.zeros((4, 128), F32)
        picked_total = jnp.zeros((4, 128), F32)
        for n in range(count):
            exp_total = exp_total + ref[n, 4:8, :] * jnp.exp(ref[n, 0:4, :] - top)
            picked_total = picked_total + ref[n, 8:12, :]
        return top, exp_total, picked_total

    wait(fs.at[0:15], asem.at[3])
    top, exp_total, picked_total = join_stats(fs, 16)
    fz[s, 0:4, :] = top
    fz[s, 4:8, :] = exp_total
    fz[s, 8:12, :] = picked_total
    fz[s, 12:16, :] = jnp.zeros((4, 128), F32)

    def send_final(k):
        send(fz.at[s], fz.at[s], bsem.at[72], asem.at[4], (c, lax.rem(s + k, 16), z))

    each(1, 16, send_final)
    wait(fz.at[0:15], asem.at[4])
    top, exp_total, picked_total = join_stats(fz, 16)
    grouped = picked_total - top - jnp.log(exp_total)
    cols = []
    for t in range(4):
        first, second = grouped[t % 2 * 2 : t % 2 * 2 + 1], grouped[t % 2 * 2 + 1 : t % 2 * 2 + 2]
        if t // 2 == 0:
            second = pltpu.roll(second, 64, 1)
        else:
            first = pltpu.roll(first, 64, 1)
        cols.append(column(jnp.where(lane[0:1] < 64, first, second)))
    for e in range(4):
        lp_ref[e : e + 1, :] = sum(
            jnp.sum(
                jnp.where(
                    place[t * 128 : (t + 1) * 128, e * 128 : (e + 1) * 128].astype(F32) > 0.0,
                    cols[t],
                    0.0,
                ),
                axis=0,
                keepdims=True,
            )
            for t in range(4)
        )

    wait(xn.at[0:496], bsem.at[0])
    wait(xn.at[0:496], bsem.at[1])
    for p in range(4):
        wait(r1.at[p], bsem.at[4 + p])
        wait(r2.at[p, 0:3], bsem.at[8 + p])
        wait(r3.at[p, 0:3], bsem.at[12 + p])
        wait(qkv.at[0:48], bsem.at[16 + p])
        wait(qkv.at[0:64], bsem.at[20 + p])
        wait(rc1.at[p], bsem.at[24 + p])
        wait(rc2.at[p, 0:3], bsem.at[32 + p])
        wait(rc3.at[p, 0:3], bsem.at[40 + p])
        wait(ho.at[0:48], bsem.at[48 + p])
        wait(ho.at[0:64], bsem.at[52 + p])
        wait(zr.at[p, 0:7], bsem.at[56 + p])
        wait(zr.at[p, 0:7], bsem.at[60 + p])
        wait(feat.at[0, 0:15, :, 0:128], bsem.at[64 + p])
    for pair in (0, 1):
        wait(racc.at[pair], bsem.at[36 + pair])
    wait(st.at[0:31], bsem.at[68])
    wait(wv_sib, bsem.at[28])
    wait(fs.at[0:15], bsem.at[70])
    wait(fz.at[0:15], bsem.at[72])


def per_device(
    x_rows,
    attn_gain,
    final_gain,
    w_query,
    w_kv,
    w_out,
    kv_cache,
    w_vocab,
    token_ids,
    cache_len,
    row_traj,
):
    entries = w_vocab.shape[1]
    spread = np.exp(np.arange(HD // 2) * (-2.0 * math.log(rope_base) / HD)).astype(np.float32)
    vmem = pl.BlockSpec(memory_space=pltpu.VMEM)
    smem = pl.BlockSpec(memory_space=pltpu.SMEM)
    hbm = pl.BlockSpec(memory_space=pl.ANY)
    dma = pltpu.SemaphoreType.DMA
    attended, logprob = pl.pallas_call(
        kernel,
        out_shape=(
            jax.ShapeDtypeStruct((64, 256), BF16),
            jax.ShapeDtypeStruct((4, 128), F32),
        ),
        in_specs=[vmem, vmem, vmem, hbm, vmem, hbm, hbm, hbm, vmem, smem, vmem, vmem],
        out_specs=(vmem, vmem),
        scratch_shapes=[
            pltpu.VMEM((256, 1024), BF16),
            pltpu.VMEM((1024, 256), BF16),
            pltpu.VMEM((4, 1024, 128), BF16),
            pltpu.VMEM((4, 256, 1024), BF16),
            pltpu.VMEM((4, 1024, 256), BF16),
            pltpu.VMEM((entries, 4096), BF16),
            pltpu.VMEM((entries, 4096), BF16),
            pltpu.VMEM((16, 8192), BF16),
            pltpu.VMEM((512, 256), BF16),
            pltpu.VMEM((512, 256), BF16),
            pltpu.VMEM((4, 16, 256), F32),
            pltpu.VMEM((512, 512), BF16),
            pltpu.VMEM((512, 512), BF16),
            pltpu.VMEM((4, 128), F32),
            pltpu.VMEM((4, 2, 16, 128), F32),
            pltpu.VMEM((512, 256), BF16),
            pltpu.VMEM((512, 1280), F32),
            pltpu.VMEM((4, 64, 1280), F32),
            pltpu.VMEM((4, 4, 16, 1280), BF16),
            pltpu.VMEM((4, 4, 16, 1280), BF16),
            pltpu.VMEM((4, 16, 1280), F32),
            pltpu.VMEM((4, 4, 16, 1280), F32),
            pltpu.VMEM((512, 1280), BF16),
            pltpu.VMEM((512, 1152), F32),
            pltpu.VMEM((4, 64, 1152), F32),
            pltpu.VMEM((4, 4, 16, 1152), BF16),
            pltpu.VMEM((4, 4, 16, 1152), BF16),
            pltpu.VMEM((4, 16, 1024), F32),
            pltpu.VMEM((4, 16, 128), F32),
            pltpu.VMEM((4, 4, 16, 1152), BF16),
            pltpu.VMEM((512, 1024), BF16),
            pltpu.VMEM((512, 256), F32),
            pltpu.VMEM((512, 256), BF16),
            pltpu.VMEM((4, 8, 16, 256), BF16),
            pltpu.VMEM((512, 256), BF16),
            pltpu.VMEM((2, 16, 256, 256), BF16),
            pltpu.VMEM((2, 2, entries, 256), F32),
            pltpu.VMEM((2, entries, 256), F32),
            pltpu.VMEM((32, 8, 128), F32),
            pltpu.VMEM((16, 16, 128), F32),
            pltpu.VMEM((16, 16, 128), F32),
            dma((5,)),
            dma((76,)),
            dma((5,)),
            dma((4,)),
            dma((16,)),
            dma((16,)),
            dma((16,)),
            dma((4,)),
            dma((4,)),
            dma((16,)),
            dma((16,)),
            dma((16,)),
            dma((4,)),
            dma((32,)),
            dma((32,)),
            dma((64,)),
            dma((64,)),
            dma((4,)),
            dma((2,)),
        ],
        compiler_params=pltpu.CompilerParams(
            collective_id=0, has_side_effects=True, vmem_limit_bytes=60 * 1024 * 1024
        ),
        cost_estimate=pl.CostEstimate(
            flops=8_000_000_000, bytes_accessed=14_000_000, transcendentals=5_000_000
        ),
    )(
        x_rows,
        attn_gain.reshape(64, 128),
        final_gain.reshape(64, 128),
        w_query,
        w_kv,
        w_out,
        kv_cache,
        w_vocab.T,
        token_ids.reshape(4, 128),
        cache_len,
        row_traj.reshape(4, 128),
        jnp.asarray(np.concatenate([spread, spread])[None]),
    )
    return attended, logprob.reshape(-1)


def solution(mesh):
    in_specs = (
        P(("side", "seq"), None),
        P(),
        P(),
        P(("side", "seq"), "tensor"),
        P(("side", "seq"), None, "tensor"),
        P("tensor", ("side", "seq")),
        P(None, None, ("side", "seq"), "tensor"),
        P(None, ("side", "seq", "tensor")),
        P(),
        P(),
        P(),
    )
    out_specs = (P("tensor", ("side", "seq")), P())
    return jax.shard_map(
        per_device, mesh=mesh, in_specs=in_specs, out_specs=out_specs, check_vma=False
    )
```
